256 devices in a mesh: bead: 16 (over z, y_hi), space: 16 (over x, y_lo, core).
Axes of the slice: x: 4, y: 4 (y_hi: 2, y_lo: 2; y = y_hi * 2 + y_lo), z: 8, core: 2. Of those that a mesh axis runs over, the one named last changes fastest.
Arguments:
- features: bfloat16 [32, 16384, 128], P('bead', 'space'), may hold values from -6 to 6
- positions: float32 [32, 3, 16384], P('bead', None, 'space'), may hold values from 0 to 32, as said below
- send_rows: int32 [16, 2, 512], P('space'), may hold values from 0 to 1023
- neighbours: int32 [8, 16384], P(None, 'space'), may hold values from 0 to 2047
- nbr_mask: int32 [8, 16384], P(None, 'space'), may hold values 0 or 1
- w_pair: bfloat16 [128], replicated, may hold values from -0.5 to 0.5
- w_in: bfloat16 [256, 512], replicated, may hold values from -0.375 to 0.375
- w_out: bfloat16 [512, 128], replicated, may hold values from -0.25 to 0.25
- omega: float32 [32], P('bead'), may hold values from 0.1 to 1.5
- q_index: int32 [3, 64], replicated, may hold values from 1 to 4
Outputs:
- new_features: bfloat16 [32, 16384, 128], P('bead', 'space')
- new_positions: float32 [32, 3, 16384], P('bead', None, 'space')
- correlation: float32 [32, 32, 64], P('bead')
The draws below stay inside these ranges and needn't reach their ends.
Inputs may be any that keep to these rules, and one draw needn't show every extreme that they name: `positions`: atom i of every bead has its first coordinate in [2 (i // 1024), 2 (i // 1024) + 2) and the other two in [0, 4).
All inputs are finite; a program needn't handle non-finite values. No bound on the sum of `nbr_mask` on one device may be relied on, other than what follows from the above.
Results may differ from the reference program's by a relative error of at most 0.0039.
Values may be sent and summed in bfloat16 or wider, within the bound.
A program may use at most 64 MiB of HBM per device.

```python
import math
import jax
import jax.numpy as jnp
from jax import lax

W = 128
HID = 512
K = 8
Q = 64
APD = 1024
G = 512
BEADS = 32
ATOMS = 16384
N_SPACE = 16


def draw_positions(key, part):
    key_x = jax.random.fold_in(key, 11)
    key_r = jax.random.fold_in(key, 12)
    offset = jax.random.uniform(key_x, (BEADS, 1, ATOMS), jnp.float32)
    slab = (jnp.arange(ATOMS) // APD).astype(jnp.float32)[None, None, :]
    first = (slab + offset) * 2.0
    rest = jax.random.uniform(key_r, (BEADS, 2, ATOMS), jnp.float32) * 4.0
    return jnp.concatenate([first, rest], axis=1).astype(jnp.float32)


def set_ends(entries, key, low, largest):
    spot = [jax.random.randint(jax.random.fold_in(key, axis), (), 0, length) for axis, length in enumerate(entries.shape)]
    longest = entries.shape.index(max(entries.shape))
    beside = spot[:longest] + [(spot[longest] + 1) % entries.shape[longest]] + spot[longest + 1:]
    return entries.at[tuple(spot)].set(low).at[tuple(beside)].set(largest)


def shard_levels(own_key, extent, shards, smallest, top_value):
    def one(position, parts):
        draws = jax.random.uniform(jax.random.fold_in(jax.random.fold_in(own_key, 6), position), (parts,), jnp.float32, smallest / len(shards), top_value / len(shards))
        return jnp.repeat(jnp.exp(draws), extent[position] // parts).reshape((-1,) + (1,) * (len(extent) - position - 1))

    loudness = one(*shards[0])
    for cut in shards[1:]:
        loudness = loudness * one(*cut)
    return loudness


def centred(key, dims, spread, most, cuts=(), held_as=jnp.bfloat16):
    entries = spread * jax.random.normal(key, dims, jnp.float32)
    if cuts:
        entries = entries * shard_levels(key, dims, cuts, -0.22, 0.18)
    return jnp.clip(entries, -most, most).astype(held_as)


def setup_inputs(seed: int = 0) -> dict:
    key_of = jax.random.split(jax.random.key(seed), 11)
    features = centred(key_of[0], (BEADS, ATOMS, W), 1.0, 6.0, ((0, 16), (1, 16)))
    positions = draw_positions(jax.random.fold_in(key_of[10], 71), 0)
    send_rows = set_ends(jax.random.randint(key_of[2], (N_SPACE, 2, G), 0, APD), jax.random.fold_in(key_of[2], 1), 0, APD - 1).astype(jnp.int32)
    neighbours = set_ends(jax.random.randint(key_of[3], (K, ATOMS), 0, APD + 2 * G), jax.random.fold_in(key_of[3], 1), 0, (APD + 2 * G) - 1).astype(jnp.int32)
    nbr_mask = set_ends((jax.random.randint(key_of[4], (K, ATOMS), 0, 4) < 3).astype(jnp.int32), jax.random.fold_in(key_of[4], 1), 0, 1)
    w_pair = centred(key_of[5], (W,), W ** -0.5, 0.5)
    w_in = centred(key_of[6], (2 * W, HID), (2 * W) ** -0.5, 0.375)
    w_out = centred(key_of[7], (HID, W), HID ** -0.5, 0.25)
    omega = jnp.clip(jnp.exp(math.log(1.5) - 2.7080502 * jax.random.uniform(key_of[8], (BEADS,), jnp.float32) ** shard_levels(key_of[8], (BEADS,), ((0, 16),), -0.2, 0.2)), 0.1, 1.5)
    q_index = set_ends(jax.random.randint(key_of[9], (3, Q), 1, 5), jax.random.fold_in(key_of[9], 1), 1, 4).astype(jnp.int32)
    return dict(features=features, positions=positions, send_rows=send_rows, neighbours=neighbours, nbr_mask=nbr_mask, w_pair=w_pair, w_in=w_in, w_out=w_out, omega=omega, q_index=q_index)


def dct_table(order):
    kk = jnp.arange(order, dtype=jnp.float32)[:, None]
    bb = jnp.arange(order, dtype=jnp.float32)[None, :]
    scale = jnp.where(kk == 0, jnp.sqrt(1.0 / order), jnp.sqrt(2.0 / order)).astype(jnp.float32)
    return (scale * jnp.cos(math.pi * kk * (bb + 0.5) / order)).astype(jnp.float32)

def reference(features, positions, send_rows, neighbours, nbr_mask, w_pair, w_in, w_out, omega, q_index):
    box = 2.0 * N_SPACE
    half = box / 2.0
    slabs = jnp.arange(N_SPACE, dtype=jnp.int32)
    lower = (slabs - 1) % N_SPACE
    upper = (slabs + 1) % N_SPACE
    own = slabs[:, None] * APD + jnp.arange(APD, dtype=jnp.int32)[None, :]
    from_lower = lower[:, None] * APD + send_rows[lower, 1, :]
    from_upper = upper[:, None] * APD + send_rows[upper, 0, :]
    ext_index = jnp.concatenate([own, from_lower, from_upper], axis=1).astype(jnp.int32)
    domain = (jnp.arange(ATOMS, dtype=jnp.int32) // APD).astype(jnp.int32)
    global_nbr = ext_index[domain[None, :], neighbours].astype(jnp.int32)
    maskf = nbr_mask.astype(jnp.float32)

    def one_bead(item):
        feats, coords = item
        strength = jnp.dot(feats, w_pair, preferred_element_type=jnp.float32)
        agg = jnp.zeros((ATOMS, feats.shape[1]), jnp.float32)
        force = jnp.zeros((3, ATOMS), jnp.float32)
        for slot in range(neighbours.shape[0]):
            idx = global_nbr[slot]
            other = coords[:, idx]
            delta = coords - other
            first = delta[0]
            first = jnp.where(first > half, first - box, jnp.where(first < -half, first + box, first))
            delta = jnp.concatenate([first[None], delta[1:]], axis=0)
            dist_sq = lax.optimization_barrier(jnp.sum(delta * delta, axis=0))
            weight = maskf[slot] / (1.0 + dist_sq / 4.0)
            agg = agg + weight[:, None] * feats[idx].astype(jnp.float32)
            force = force + (weight * (strength + strength[idx]))[None, :] * delta
        joined = jnp.concatenate([feats, agg.astype(jnp.bfloat16)], axis=1)
        hidden = jax.nn.silu(jnp.dot(joined, w_in, preferred_element_type=jnp.float32)).astype(jnp.bfloat16)
        updated = (feats.astype(jnp.float32) + jnp.dot(hidden, w_out, preferred_element_type=jnp.float32)).astype(jnp.bfloat16)
        return (updated, force)
    new_features, forces = lax.map(one_bead, (features, positions))
    table = dct_table(BEADS)
    stacked = jnp.concatenate([positions, forces], axis=1)
    modes = jnp.einsum('kb,bca->kca', table, stacked, precision=lax.Precision.HIGHEST)
    rotated = jnp.cos(omega)[:, None, None] * modes[:, :3] + jnp.sin(omega)[:, None, None] * modes[:, 3:]
    new_positions = jnp.einsum('kb,kca->bca', table, rotated, precision=lax.Precision.HIGHEST)
    lengths = jnp.array([box, 4.0, 4.0], dtype=jnp.float32)
    qvec = 2.0 * math.pi * q_index.astype(jnp.float32) / lengths[:, None]

    def factors(coords):
        phase = jnp.einsum('cq,ca->qa', qvec, coords, precision=lax.Precision.HIGHEST)
        return jnp.stack([lax.optimization_barrier(jnp.sum(jnp.cos(phase), axis=1)), lax.optimization_barrier(jnp.sum(jnp.sin(phase), axis=1))], axis=0)
    sfac = lax.map(factors, new_positions)
    columns = []
    for lag in range(BEADS):
        rolled = jnp.roll(sfac, -lag, axis=0)
        columns.append(lax.optimization_barrier(jnp.sum(sfac * rolled, axis=1)) / ATOMS)
    correlation = jnp.stack(columns, axis=1)
    return (new_features, new_positions, correlation)
```

```python
import functools
import math

import jax
import jax.numpy as jnp
import numpy as np
from jax import lax
from jax.experimental import pallas as pl
from jax.experimental.pallas import tpu as pltpu
from jax.sharding import PartitionSpec as P

MESH = pl.DeviceIdType.MESH
F32 = jnp.float32
BF16 = jnp.bfloat16
HIGHEST = lax.Precision.HIGHEST
N = 16
APD = 1024
GHOST = 512
EXT = 2048
W = 128
SLOTS = 8
TILE = 256
BOX = 32.0


def dct_matrix(order):
    k = np.arange(order)[:, None]
    b = np.arange(order)[None, :]
    scale = np.where(k == 0, np.sqrt(1.0 / order), np.sqrt(2.0 / order))
    return scale * np.cos(math.pi * k * (b + 0.5) / order)


def mode_tables():
    c = dct_matrix(32)
    forward = np.zeros((224, 256), np.float32)
    backward = np.zeros((96, 96), np.float32)
    ids = np.arange(N)
    for h in range(2):
        for kind in range(2):
            for comp in range(3):
                rows = 96 * h + 48 * kind + 16 * comp + ids
                for half in range(2):
                    par = h if half == 0 else 1 - h
                    cols = 128 * half + 8 * ids + 3 * kind + comp
                    forward[np.ix_(rows, cols)] = c[np.ix_(2 * ids + h, 2 * ids + par)]
        for comp in range(3):
            rows = 48 * h + 16 * comp + ids
            for half in range(2):
                par = h if half == 0 else 1 - h
                cols = 48 * half + 16 * comp + ids
                backward[np.ix_(rows, cols)] = c[np.ix_(2 * ids + par, 2 * ids + h)].T
    forward[192 + ids, 8 * ids + 6] = 1.0
    forward[208 + ids, 8 * ids + 7] = 1.0
    return forward, backward


def other(axis, offset):
    return {axis: lax.rem(lax.axis_index(axis) + offset, N)}


def lane_gather(row, index):
    return jnp.take_along_axis(row, index, axis=1, mode="promise_in_bounds")


def cos_turns(t):
    t = t - jnp.round(t)
    s = t * t
    u = s * (4.0 * math.pi * math.pi / 16.0)
    c = 1.0 + u * (-0.5 + u * (1.0 / 24 + u * (-1.0 / 720 + u * (1.0 / 40320 - u / 3628800))))
    m = c - 1.0
    m = 2.0 * m * (m + 2.0)
    m = 2.0 * m * (m + 2.0)
    return 1.0 + m


def kernel(
    feats,
    pos,
    send,
    nbr,
    mask,
    w_pair,
    w_in,
    w_out,
    omega,
    q_index,
    forward,
    backward,
    new_feats,
    new_pos,
    corr,
    table,
    small_out,
    ghost_out,
    ghost_in,
    coeff,
    columns,
    dense,
    beadrow,
    mode_out,
    mode_in,
    back_out,
    back_in,
    sum_out,
    sum_in,
    all_in,
    small_send,
    small_recv,
    ghost_send,
    ghost_recv,
    mode_send,
    mode_recv,
    back_send,
    back_recv,
    sum_send,
    sum_recv,
    all_send,
    all_recv,
):
    bead = lax.axis_index("bead")
    space = lax.axis_index("space")
    barrier = pltpu.get_barrier_semaphore()
    for axis in ("bead", "space"):
        for o in range(1, N):
            pl.semaphore_signal(barrier, inc=1, device_id=other(axis, o), device_id_type=MESH)

    lane = lax.broadcasted_iota(jnp.int32, (8, 128), 1)
    low_half = lane < 64

    pair_rows = jnp.broadcast_to(w_pair[...], (16, W))
    for b in range(2):
        strength = lax.dot_general(
            pair_rows, feats[b], (((1,), (1,)), ((), ())), preferred_element_type=F32
        )
        table[4 * b : 4 * b + 3, 0:APD] = pos[b]
        table[4 * b + 3 : 4 * b + 4, 0:APD] = strength[0:1]
        beadrow[b, 0:3] = pos[b]
        om = jnp.full((1, APD), omega[b], F32)
        beadrow[b, 6:7] = jnp.cos(om)
        beadrow[b, 7:8] = jnp.sin(om)

    for side in range(2):
        for blk in range(4):
            idx = jnp.broadcast_to(send[0, side : side + 1, 128 * blk : 128 * blk + 128], (8, 128))
            hi = lax.shift_right_logical(idx, 7)
            lo = lax.bitwise_and(idx, 127)
            acc = jnp.zeros((8, 128), F32)
            for h in range(8):
                got = lane_gather(table[:, 128 * h : 128 * h + 128], lo)
                acc = jnp.where(hi == h, got, acc)
            small_out[side, :, 128 * blk : 128 * blk + 128] = acc

    pl.semaphore_wait(barrier, 2 * (N - 1))

    small = []
    for side, step in ((0, N - 1), (1, 1)):
        start = APD + GHOST if side == 0 else APD
        copy = pltpu.make_async_remote_copy(
            src_ref=small_out.at[side],
            dst_ref=table.at[:, pl.ds(start, GHOST)],
            send_sem=small_send.at[side],
            recv_sem=small_recv.at[side],
            device_id=other("space", step),
            device_id_type=MESH,
        )
        copy.start()
        small.append(copy)

    both = jnp.concatenate([feats[0], feats[1]], axis=1)
    wide = lax.broadcasted_iota(jnp.int32, (128, APD), 1)
    ghosts = []
    for side, step in ((0, N - 1), (1, 1)):
        for blk in range(4):
            idx = jnp.broadcast_to(
                send[0, side : side + 1, 128 * blk : 128 * blk + 128], (128, 128)
            )
            col = jnp.transpose(idx)[:, 0:1]
            hot = (col == wide).astype(F32).astype(BF16)
            rows = jnp.dot(hot, both, preferred_element_type=F32).astype(BF16)
            ghost_out[side, 0, 128 * blk : 128 * blk + 128] = rows[:, 0:W]
            ghost_out[side, 1, 128 * blk : 128 * blk + 128] = rows[:, W:]
        copy = pltpu.make_async_remote_copy(
            src_ref=ghost_out.at[side],
            dst_ref=ghost_in.at[1 - side],
            send_sem=ghost_send.at[side],
            recv_sem=ghost_recv.at[side],
            device_id=other("space", step),
            device_id_type=MESH,
        )
        copy.start()
        ghosts.append(copy)

    for copy in small:
        copy.wait_recv()

    def block(blk, _):
        at = pl.ds(pl.multiple_of(blk * 128, 128), 128)
        idx = nbr[:, at]
        live = mask[:, at].astype(F32)
        hi = lax.shift_right_logical(idx, 7)
        lo = lax.bitwise_and(idx, 127)
        picked = [jnp.zeros((8, 128), F32) for _ in range(8)]
        for h in range(EXT // 128):
            hit = hi == h
            for q in range(8):
                row = jnp.broadcast_to(table[q : q + 1, 128 * h : 128 * h + 128], (8, 128))
                picked[q] = jnp.where(hit, lane_gather(row, lo), picked[q])
        code = (128 + lo).astype(F32) * lax.shift_left(jnp.ones_like(hi), hi).astype(F32)
        cs = []
        for b in range(2):
            d = []
            for c in range(3):
                d.append(table[4 * b + c : 4 * b + c + 1, at] - picked[4 * b + c])
            first = d[0]
            first = jnp.where(
                first > BOX / 2,
                first - BOX,
                jnp.where(first < -BOX / 2, first + BOX, first),
            )
            d[0] = first
            dist = d[0] * d[0] + d[1] * d[1] + d[2] * d[2]
            weight = live / (1.0 + dist / 4.0)
            pair = weight * (table[4 * b + 3 : 4 * b + 4, at] + picked[4 * b + 3])
            for c in range(3):
                beadrow[b, 3 + c : 4 + c, at] = jnp.sum(pair * d[c], axis=0, keepdims=True)
            cs.append(weight)
        total = list(cs)
        for r in range(1, SLOTS):
            same = pltpu.roll(idx, r, 0) == idx
            for b in range(2):
                total[b] = total[b] + jnp.where(same, pltpu.roll(cs[b], r, 0), 0.0)
        stack = jnp.concatenate(
            [code, total[0], total[1], jnp.zeros((104, 128), F32)], axis=0
        )
        columns[at, :] = jnp.transpose(stack)
        one = beadrow[0, :, at]
        two = beadrow[1, :, at]
        mode_out[2 * blk] = jnp.where(low_half, one, pltpu.roll(two, 64, 1))
        mode_out[2 * blk + 1] = jnp.where(low_half, pltpu.roll(one, 64, 1), two)
        return 0

    lax.fori_loop(0, APD // 128, block, 0)

    def exchange(axis, source, target, send_sem, recv_sem):
        me = lax.axis_index(axis)
        copies = []
        for o in range(1, N):
            to = lax.rem(me + o, N)
            copy = pltpu.make_async_remote_copy(
                src_ref=source(to),
                dst_ref=target(me, N - o),
                send_sem=send_sem.at[o],
                recv_sem=recv_sem.at[N - o],
                device_id={axis: to},
                device_id_type=MESH,
            )
            copy.start()
            copies.append(copy)
        return copies

    mode_copies = exchange(
        "bead", lambda to: mode_out.at[to], lambda me, r: mode_in.at[me], mode_send, mode_recv
    )
    mode_in[bead] = mode_out[bead]
    for copy in ghosts:
        copy.wait_recv()

    lane_code = (128 + lax.broadcasted_iota(jnp.int32, (16, 128), 1)).astype(F32)

    def dense_tile(t):
        def strip(s, _):
            at = pl.ds(pl.multiple_of(t * TILE + s * 16, 16), 16)
            cols = columns[at, :]

            def spread(j):
                return jnp.broadcast_to(cols[:, j : j + 1], (16, 128)).astype(BF16)

            codes = [spread(k) for k in range(SLOTS)]
            c0 = [spread(8 + k) for k in range(SLOTS)]
            c1 = [spread(16 + k) for k in range(SLOTS)]
            row = pl.ds(pl.multiple_of(s * 16, 16), 16)
            for h in range(EXT // 128):
                here = (lane_code * float(2**h)).astype(BF16)
                a0 = jnp.zeros((16, 128), BF16)
                a1 = jnp.zeros((16, 128), BF16)
                for k in range(SLOTS):
                    hit = codes[k] == here
                    a0 = jnp.where(hit, c0[k], a0)
                    a1 = jnp.where(hit, c1[k], a1)
                dense[0, row, 128 * h : 128 * h + 128] = a0
                dense[1, row, 128 * h : 128 * h + 128] = a1
            return 0

        lax.fori_loop(0, TILE // 16, strip, 0)
        at = pl.ds(pl.multiple_of(t * TILE, TILE), TILE)
        for b in range(2):
            agg = jnp.dot(dense[b, :, 0:APD], feats[b], preferred_element_type=F32)
            agg += jnp.dot(
                dense[b, :, APD : APD + GHOST], ghost_in[0, b], preferred_element_type=F32
            )
            agg += jnp.dot(dense[b, :, APD + GHOST :], ghost_in[1, b], preferred_element_type=F32)
            mine = feats[b, at, :]
            joined = jnp.concatenate([mine, agg.astype(BF16)], axis=1)
            x = jnp.dot(joined, w_in[...], preferred_element_type=F32)
            hidden = (x * (0.5 * (1.0 + jnp.tanh(0.5 * x)))).astype(BF16)
            out = mine.astype(F32) + jnp.dot(hidden, w_out[...], preferred_element_type=F32)
            new_feats[b, at, :] = out.astype(BF16)

    def dense_tiles(first, last):
        def step(t, _):
            dense_tile(t)
            return 0

        lax.fori_loop(first, last, step, 0)

    dense_tiles(0, 1)

    for copy in mode_copies:
        copy.wait_recv()
    low = lax.broadcasted_iota(jnp.int32, (48, 128), 1) < 64
    z = mode_in[...].reshape(128, 128)
    z = jnp.concatenate([z, pltpu.roll(z, 64, 1)], axis=0)
    y = jnp.dot(forward[...], z, precision=HIGHEST, preferred_element_type=F32)
    cosw = jnp.concatenate([y[192:208]] * 3, axis=0)
    sinw = jnp.concatenate([y[208:224]] * 3, axis=0)
    rotated = cosw * jnp.where(low, y[0:48], y[96:144]) + sinw * jnp.where(
        low, y[48:96], y[144:192]
    )
    z = jnp.concatenate([rotated, pltpu.roll(rotated, 64, 1)], axis=0)
    y = jnp.dot(backward[...], z, precision=HIGHEST, preferred_element_type=F32)
    moved = jnp.where(low, y[0:48], y[48:96])
    for d in range(N):
        for c in range(3):
            back_out[d, c : c + 1] = moved[16 * c + d : 16 * c + d + 1]
    back_copies = exchange(
        "bead", lambda to: back_out.at[to], lambda me, r: back_in.at[me], back_send, back_recv
    )
    back_in[bead] = back_out[bead]

    dense_tiles(1, 2)

    q0 = q_index[0:1, :]
    pick = 4 * (q_index[1:2, :] - 1) + (q_index[2:3, :] - 1)
    pick = jnp.concatenate([pick, pick + 16], axis=1)
    q0 = jnp.concatenate([q0, q0], axis=1)
    row64 = lax.broadcasted_iota(jnp.int32, (64, 128), 0)
    choose = (lax.bitwise_and(row64, 31) == pick).astype(F32)
    row16 = lax.broadcasted_iota(jnp.int32, (16, 128), 0)
    row8 = lax.bitwise_and(row16, 7)
    lane16 = lax.broadcasted_iota(jnp.int32, (16, 128), 1)
    direct = (row8 == q0 - 1).astype(F32)
    crossed = jnp.where(row8 == q0 + 3, jnp.where(lane16 < 64, -1.0, 1.0), 0.0)

    for copy in back_copies:
        copy.wait_recv()
    for m in range(8):
        one = back_in[2 * m]
        two = back_in[2 * m + 1]
        at = slice(128 * m, 128 * m + 128)
        first = jnp.where(low_half, one, pltpu.roll(two, 64, 1))
        second = jnp.where(low_half, pltpu.roll(one, 64, 1), two)
        new_pos[0, :, at] = first[0:3]
        new_pos[1, :, at] = second[0:3]

    r8 = lax.broadcasted_iota(jnp.int32, (8, APD), 0)
    r32 = lax.broadcasted_iota(jnp.int32, (32, APD), 0)
    u_q = (lax.bitwise_and(r8, 3) + 1).astype(F32) * (1.0 / BOX)
    u_off = jnp.where(r8 >= 4, 0.25, 0.0)
    v_q1 = (lax.bitwise_and(lax.shift_right_logical(r32, 2), 3) + 1).astype(F32) * 0.25
    v_q2 = (lax.bitwise_and(r32, 3) + 1).astype(F32) * 0.25
    v_off = jnp.where(r32 >= 16, 0.25, 0.0)
    us, vs = [], []
    for b in range(2):
        us.append(cos_turns(u_q * new_pos[b, 0:1, :] - u_off))
        vs.append(cos_turns(v_q1 * new_pos[b, 1:2, :] + v_q2 * new_pos[b, 2:3, :] - v_off))
    raw = lax.dot_general(
        jnp.concatenate(us, axis=0),
        jnp.concatenate(vs, axis=0),
        (((1,), (1,)), ((), ())),
        precision=HIGHEST,
        preferred_element_type=F32,
    )
    own_row = lax.broadcasted_iota(jnp.int32, (16, 64), 0) < 8
    own_col = lax.broadcasted_iota(jnp.int32, (16, 64), 1) < 32
    raw = jnp.where(own_row == own_col, raw, 0.0)
    spread_q = jnp.dot(raw, choose, precision=HIGHEST, preferred_element_type=F32)
    parts = direct * spread_q + crossed * pltpu.roll(spread_q, 64, 1)
    sum_out[0:1] = jnp.sum(parts[0:8], axis=0, keepdims=True)
    sum_out[1:2] = jnp.sum(parts[8:16], axis=0, keepdims=True)

    sum_copies = exchange(
        "space", lambda to: sum_out, lambda me, r: sum_in.at[r], sum_send, sum_recv
    )
    dense_tiles(2, 3)
    for copy in sum_copies:
        copy.wait_recv()
    total = sum_out[...]
    for r in range(1, N):
        total = total + sum_in[r]
    all_in[0] = total
    all_copies = exchange(
        "bead", lambda to: all_in.at[0], lambda me, r: all_in.at[r], all_send, all_recv
    )
    dense_tiles(3, 4)
    for copy in all_copies:
        copy.wait_recv()
    every = jnp.concatenate([all_in[r] for r in range(N)], axis=0)
    for b in range(2):
        prod = every * (every[b : b + 1] * (1.0 / (APD * N)))
        both_q = prod + pltpu.roll(prod, 64, 1)
        if b:
            both_q = jnp.concatenate([both_q[1:], both_q[0:1]], axis=0)
        corr[b] = both_q[:, 0:64]

    for copy in small + ghosts + mode_copies + back_copies + sum_copies + all_copies:
        copy.wait_send()


def on_device(
    features, positions, send_rows, neighbours, nbr_mask, w_pair, w_in, w_out, omega, q_index
):
    forward, backward = mode_tables()
    vmem = pl.BlockSpec(memory_space=pltpu.VMEM)
    smem = pl.BlockSpec(memory_space=pltpu.SMEM)
    dma = pltpu.SemaphoreType.DMA
    return pl.pallas_call(
        kernel,
        out_shape=(
            jax.ShapeDtypeStruct((2, APD, W), BF16),
            jax.ShapeDtypeStruct((2, 3, APD), F32),
            jax.ShapeDtypeStruct((2, 32, 64), F32),
        ),
        in_specs=[vmem] * 8 + [smem] + [vmem] * 3,
        out_specs=(vmem, vmem, vmem),
        scratch_shapes=[
            pltpu.VMEM((8, EXT), F32),
            pltpu.VMEM((2, 8, GHOST), F32),
            pltpu.VMEM((2, 2, GHOST, W), BF16),
            pltpu.VMEM((2, 2, GHOST, W), BF16),
            pltpu.VMEM((8, 128), F32),
            pltpu.VMEM((APD, 128), F32),
            pltpu.VMEM((2, TILE, EXT), BF16),
            pltpu.VMEM((2, 8, APD), F32),
            pltpu.VMEM((N, 8, 128), F32),
            pltpu.VMEM((N, 8, 128), F32),
            pltpu.VMEM((N, 8, 128), F32),
            pltpu.VMEM((N, 8, 128), F32),
            pltpu.VMEM((2, 128), F32),
            pltpu.VMEM((N, 2, 128), F32),
            pltpu.VMEM((N, 2, 128), F32),
            dma((2,)),
            dma((2,)),
            dma((2,)),
            dma((2,)),
        ]
        + [dma((N,))] * 8,
        compiler_params=pltpu.CompilerParams(
            collective_id=0, has_side_effects=True, vmem_limit_bytes=48 * 2**20
        ),
    )(
        features,
        positions,
        send_rows,
        neighbours,
        nbr_mask,
        w_pair.reshape(1, W),
        w_in,
        w_out,
        omega,
        q_index,
        jnp.asarray(forward),
        jnp.asarray(backward),
    )


def solution(mesh):
    in_specs = (
        P("bead", "space", None),
        P("bead", None, "space"),
        P("space", None, None),
        P(None, "space"),
        P(None, "space"),
        P(),
        P(),
        P(),
        P("bead"),
        P(),
    )
    out_specs = (P("bead", "space", None), P("bead", None, "space"), P("bead", None, None))
    return jax.shard_map(
        on_device, mesh=mesh, in_specs=in_specs, out_specs=out_specs, check_vma=False
    )
```

```python
import functools
import math

import jax
import jax.numpy as jnp
from jax import lax
from jax.experimental import pallas as pl
from jax.experimental.pallas import tpu as pltpu
from jax.sharding import PartitionSpec as P

MESH = pl.DeviceIdType.MESH
F32 = jnp.float32
BF16 = jnp.bfloat16
HIGHEST = lax.Precision.HIGHEST
N = 16
RING = 8
APD = 1024
GHOST = 512
EXT = 2048
W = 128
SLOTS = 8
TILE = 256
BOX = 32.0


def other(axis, offset):
    return {axis: lax.rem(lax.axis_index(axis) + offset, N)}


def lane_gather(row, index):
    return jnp.take_along_axis(row, index, axis=1, mode="promise_in_bounds")


def cos_turns(t):
    t = t - jnp.round(t)
    u = (t * t) * (math.pi * math.pi / 4.0)
    m = u * (-0.5 + u * (1.0 / 24 + u * (-1.0 / 720 + u * (1.0 / 40320 - u / 3628800))))
    m = 2.0 * m * (m + 2.0)
    m = 2.0 * m * (m + 2.0)
    return 1.0 + m


def dct_entry(k, bead):
    turns = lax.bitwise_and(k * (2 * bead + 1), 127).astype(F32) * (1.0 / 128.0)
    return jnp.where(k == 0, math.sqrt(1.0 / 32), math.sqrt(2.0 / 32)) * cos_turns(turns)


def kernel(
    feats_hbm,
    pos_hbm,
    send_hbm,
    nbr_hbm,
    mask_hbm,
    w_pair_hbm,
    w_in_hbm,
    w_out_hbm,
    omega_hbm,
    q_hbm,
    new_feats,
    new_pos,
    corr,
    feats,
    pos,
    send,
    nbr,
    mask,
    w_pair,
    w_in,
    w_out,
    omega,
    q_index,
    load_sem,
    table,
    small_out,
    ghost_out,
    ghost_in,
    columns,
    dense,
    pos_out,
    pos_in,
    force_out,
    force_in,
    waves,
    coeff,
    moved,
    moved_in,
    sum_in,
    all_in,
    small_send,
    small_recv,
    ghost_send,
    ghost_recv,
    pos_send,
    pos_recv,
    force_send,
    force_recv,
    moved_sem,
    sum_send,
    sum_recv,
    all_send,
    all_recv,
):
    bead = lax.axis_index("bead")
    space = lax.axis_index("space")
    ring = lax.div(bead, 2)
    half = lax.rem(bead, 2)
    barrier = pltpu.get_barrier_semaphore()

    def plane(side, step):
        return {
            "bead": 2 * ring + lax.rem(half + side, 2),
            "space": lax.rem(space + step, N),
        }

    for step in (1, N - 1) + tuple(range(2, N - 1)):
        pl.semaphore_signal(barrier, inc=1, device_id=plane(0, step), device_id_type=MESH)
    for step in range(N):
        pl.semaphore_signal(barrier, inc=1, device_id=plane(1, step), device_id_type=MESH)
    for step in range(1, RING):
        for side in range(2):
            to = 2 * lax.rem(ring + step, RING) + side
            pl.semaphore_signal(barrier, inc=1, device_id={"bead": to}, device_id_type=MESH)
    partners = (N - 1) + N + 2 * (RING - 1)

    loads = []
    for source, target in (
        (w_pair_hbm, w_pair),
        (feats_hbm, feats),
        (pos_hbm, pos),
        (send_hbm, send),
        (nbr_hbm, nbr),
        (mask_hbm, mask),
        (omega_hbm, omega),
        (w_in_hbm, w_in),
        (w_out_hbm, w_out),
        (q_hbm, q_index),
    ):
        copy = pltpu.make_async_copy(source, target, load_sem.at[len(loads)])
        copy.start()
        loads.append(copy)

    lane = lax.broadcasted_iota(jnp.int32, (8, 128), 1)

    for i in range(4):
        loads[i].wait()
    pair_rows = jnp.broadcast_to(w_pair[...], (16, W))
    for b in range(2):
        strength = lax.dot_general(
            pair_rows, feats[b], (((1,), (1,)), ((), ())), preferred_element_type=F32
        )
        for c in range(3):
            table[4 * b + c : 4 * b + c + 1, 0:APD] = pos[c, b : b + 1]
        table[4 * b + 3 : 4 * b + 4, 0:APD] = strength[0:1]

    for side in range(2):
        for blk in range(4):
            idx = jnp.broadcast_to(send[0, side : side + 1, 128 * blk : 128 * blk + 128], (8, 128))
            hi = lax.shift_right_logical(idx, 7)
            lo = lax.bitwise_and(idx, 127)
            acc = jnp.zeros((8, 128), F32)
            for h in range(8):
                got = lane_gather(table[:, 128 * h : 128 * h + 128], lo)
                acc = jnp.where(hi == h, got, acc)
            small_out[side, :, 128 * blk : 128 * blk + 128] = acc

    for i in range(4, 7):
        loads[i].wait()
    for part in range(2):
        for c in range(3):
            for b in range(2):
                for blk in range(4):
                    at = GHOST * part + 128 * blk
                    row = 8 * c + 4 * b + blk
                    pos_out[part, row : row + 1] = pos[c, b : b + 1, at : at + 128]
    angle = jnp.concatenate([jnp.full((1, 128), omega[b], F32) for b in range(2)], axis=0)
    wave_rows = jnp.concatenate([jnp.cos(angle), jnp.sin(angle), jnp.zeros((4, 128), F32)], axis=0)
    for part in range(2):
        pos_out[part, 24:32] = wave_rows

    pl.semaphore_wait(barrier, partners)

    def to_neighbour(source, target, send_sem, recv_sem, side):
        copy = pltpu.make_async_remote_copy(
            src_ref=source,
            dst_ref=target,
            send_sem=send_sem.at[side],
            recv_sem=recv_sem.at[side],
            device_id=other("space", N - 1 if side == 0 else 1),
            device_id_type=MESH,
        )
        copy.start()
        return copy

    small = []
    for side in range(2):
        start = APD + GHOST if side == 0 else APD
        small.append(
            to_neighbour(
                small_out.at[side], table.at[:, pl.ds(start, GHOST)], small_send, small_recv, side
            )
        )

    def to_beads(source, target, send_sem, recv_sem, offsets):
        copies = []
        for o in offsets:
            to = lax.rem(bead + o, N)
            copy = pltpu.make_async_remote_copy(
                src_ref=source.at[lax.rem(to, 2)],
                dst_ref=target.at[bead],
                send_sem=send_sem.at[o],
                recv_sem=recv_sem.at[N - o],
                device_id={"bead": to},
                device_id_type=MESH,
            )
            copy.start()
            copies.append(copy)
        return copies

    crossing = (7, 9, 5, 11, 3, 13, 1, 15)
    straight = (8, 6, 10, 4, 12, 2, 14)
    pos_copies = to_beads(pos_out, pos_in, pos_send, pos_recv, crossing + straight)
    pos_in[bead] = pos_out[half]

    both = jnp.concatenate([feats[0], feats[1]], axis=1)
    wide = lax.broadcasted_iota(jnp.int32, (128, APD), 1)
    ghosts = []
    for side in range(2):
        for blk in range(4):
            idx = jnp.broadcast_to(
                send[0, side : side + 1, 128 * blk : 128 * blk + 128], (128, 128)
            )
            col = jnp.transpose(idx)[:, 0:1]
            hot = (col == wide).astype(F32).astype(BF16)
            rows = jnp.dot(hot, both, preferred_element_type=F32).astype(BF16)
            ghost_out[side, 0, 128 * blk : 128 * blk + 128] = rows[:, 0:W]
            ghost_out[side, 1, 128 * blk : 128 * blk + 128] = rows[:, W:]
        ghosts.append(
            to_neighbour(ghost_out.at[side], ghost_in.at[1 - side], ghost_send, ghost_recv, side)
        )

    for copy in small:
        copy.wait_recv()

    def block(part, blk):
        at = pl.ds(pl.multiple_of(GHOST * part + 128 * blk, 128), 128)
        idx = nbr[:, at]
        live = mask[:, at].astype(F32)
        hi = lax.shift_right_logical(idx, 7)
        lo = lax.bitwise_and(idx, 127)
        picked = [jnp.zeros((8, 128), F32) for _ in range(8)]
        for h in range(EXT // 128):
            hit = hi == h
            for q in range(8):
                row = jnp.broadcast_to(table[q : q + 1, 128 * h : 128 * h + 128], (8, 128))
                picked[q] = jnp.where(hit, lane_gather(row, lo), picked[q])
        code = (128 + lo).astype(F32) * lax.shift_left(jnp.ones_like(hi), hi).astype(F32)
        cs = []
        for b in range(2):
            d = []
            for c in range(3):
                d.append(table[4 * b + c : 4 * b + c + 1, at] - picked[4 * b + c])
            first = d[0]
            d[0] = jnp.where(
                first > BOX / 2,
                first - BOX,
                jnp.where(first < -BOX / 2, first + BOX, first),
            )
            dist = d[0] * d[0] + d[1] * d[1] + d[2] * d[2]
            weight = live / (1.0 + dist / 4.0)
            pair = weight * (table[4 * b + 3 : 4 * b + 4, at] + picked[4 * b + 3])
            for c in range(3):
                row = pl.ds(8 * c + 4 * b + blk, 1)
                force_out[part, row, :] = jnp.sum(pair * d[c], axis=0, keepdims=True)
            cs.append(weight)
        total = list(cs)
        for r in range(1, SLOTS):
            same = pltpu.roll(idx, r, 0) == idx
            for b in range(2):
                total[b] = total[b] + jnp.where(same, pltpu.roll(cs[b], r, 0), 0.0)
        stack = jnp.concatenate([code, total[0], total[1], jnp.zeros((104, 128), F32)], axis=0)
        columns[at, :] = jnp.transpose(stack)

    def blocks(part):
        def step(blk, _):
            block(part, blk)
            return 0

        lax.fori_loop(0, 4, step, 0)

    blocks(1 - half)
    force_copies = to_beads(force_out, force_in, force_send, force_recv, crossing)
    blocks(half)
    force_copies += to_beads(force_out, force_in, force_send, force_recv, straight)
    force_in[bead] = force_out[half]

    for copy in pos_copies:
        copy.wait_recv()
    for source in range(N):
        waves[0, 2 * source : 2 * source + 2] = pos_in[source, 24:26]
        waves[1, 2 * source : 2 * source + 2] = pos_in[source, 26:28]
    k_rows = lax.broadcasted_iota(jnp.int32, (32, 128), 0)
    by_mode = []
    for e in range(4):
        entry = dct_entry(k_rows, 4 * ring + e)
        by_mode += [entry * waves[0], entry * waves[1]]
    rows = lax.broadcasted_iota(jnp.int32, (128, 32), 0)
    source_bead = 2 * lax.shift_right_logical(rows, 3) + lax.bitwise_and(
        lax.shift_right_logical(rows, 2), 1
    )
    spread = dct_entry(lax.broadcasted_iota(jnp.int32, (128, 32), 1), source_bead)
    coeff[...] = jnp.dot(
        spread,
        jnp.concatenate(by_mode, axis=1),
        precision=HIGHEST,
        preferred_element_type=F32,
    )

    def mix(kind, data, acc):
        for source in range(N):
            for c in range(3):
                value = data[source, 8 * c : 8 * c + 8]
                for e in range(4):
                    lanes = slice(128 * (2 * e + kind), 128 * (2 * e + kind) + 128)
                    acc[3 * e + c] = acc[3 * e + c] + coeff[8 * source : 8 * source + 8, lanes] * value
        return acc

    acc = mix(0, pos_in, [jnp.zeros((8, 128), F32) for _ in range(12)])

    for i in range(7, 10):
        loads[i].wait()
    for copy in ghosts:
        copy.wait_recv()

    lane_code = (128 + lax.broadcasted_iota(jnp.int32, (16, 128), 1)).astype(F32)

    def dense_tile(t):
        def strip(s, _):
            at = pl.ds(pl.multiple_of(t * TILE + s * 16, 16), 16)
            cols = columns[at, :]

            def spread_lane(j):
                return jnp.broadcast_to(cols[:, j : j + 1], (16, 128)).astype(BF16)

            codes = [spread_lane(k) for k in range(SLOTS)]
            c0 = [spread_lane(8 + k) for k in range(SLOTS)]
            c1 = [spread_lane(16 + k) for k in range(SLOTS)]
            row = pl.ds(pl.multiple_of(s * 16, 16), 16)
            for h in range(EXT // 128):
                here = (lane_code * float(2**h)).astype(BF16)
                a0 = jnp.zeros((16, 128), BF16)
                a1 = jnp.zeros((16, 128), BF16)
                for k in range(SLOTS):
                    hit = codes[k] == here
                    a0 = jnp.where(hit, c0[k], a0)
                    a1 = jnp.where(hit, c1[k], a1)
                dense[0, row, 128 * h : 128 * h + 128] = a0
                dense[1, row, 128 * h : 128 * h + 128] = a1
            return 0

        lax.fori_loop(0, TILE // 16, strip, 0)
        at = pl.ds(pl.multiple_of(t * TILE, TILE), TILE)
        for b in range(2):
            agg = jnp.dot(dense[b, :, 0:APD], feats[b], preferred_element_type=F32)
            agg += jnp.dot(
                dense[b, :, APD : APD + GHOST], ghost_in[0, b], preferred_element_type=F32
            )
            agg += jnp.dot(dense[b, :, APD + GHOST :], ghost_in[1, b], preferred_element_type=F32)
            mine = feats[b, at, :]
            joined = jnp.concatenate([mine, agg.astype(BF16)], axis=1)
            x = jnp.dot(joined, w_in[...], preferred_element_type=F32)
            hidden = (x * (0.5 * (1.0 + jnp.tanh(0.5 * x)))).astype(BF16)
            out = mine.astype(F32) + jnp.dot(hidden, w_out[...], preferred_element_type=F32)
            new_feats[b, at, :] = out.astype(BF16)

    def dense_tiles(first, last):
        def step(t, _):
            dense_tile(t)
            return 0

        lax.fori_loop(first, last, step, 0)

    dense_tiles(0, 1)

    q0 = q_index[0:1, :]
    pick = 4 * (q_index[1:2, :] - 1) + (q_index[2:3, :] - 1)
    pick = jnp.concatenate([pick, pick + 16], axis=1)
    q0 = jnp.concatenate([q0, q0], axis=1)
    row128 = lax.broadcasted_iota(jnp.int32, (128, 128), 0)
    choose = (lax.bitwise_and(row128, 31) == pick).astype(F32)
    row32 = lax.broadcasted_iota(jnp.int32, (32, 128), 0)
    lane32 = lax.broadcasted_iota(jnp.int32, (32, 128), 1)
    row8 = lax.bitwise_and(row32, 7)
    direct = (row8 == q0 - 1).astype(F32)
    crossed = jnp.where(row8 == q0 + 3, jnp.where(lane32 < 64, -1.0, 1.0), 0.0)
    same_bead = lax.shift_right_logical(row32, 3) == lax.shift_right_logical(lane32, 5)
    r8 = lax.broadcasted_iota(jnp.int32, (8, 128), 0)
    u_q = (lax.bitwise_and(r8, 3) + 1).astype(F32) * (1.0 / BOX)
    u_off = jnp.where(r8 >= 4, 0.25, 0.0)
    v_q1 = (lax.bitwise_and(lax.shift_right_logical(row32, 2), 3) + 1).astype(F32) * 0.25
    v_q2 = (lax.bitwise_and(row32, 3) + 1).astype(F32) * 0.25
    v_off = jnp.where(row32 >= 16, 0.25, 0.0)

    for copy in force_copies:
        copy.wait_recv()
    acc = mix(1, force_in, acc)
    for e in range(4):
        for c in range(3):
            row = 8 * c + 4 * (e % 2)
            value = acc[3 * e + c]
            moved[e // 2, row : row + 4] = (value + pltpu.roll(value, 4, 0))[0:4]
    moved_copy = pltpu.make_async_remote_copy(
        src_ref=moved.at[1 - half],
        dst_ref=moved_in,
        send_sem=moved_sem.at[0],
        recv_sem=moved_sem.at[1],
        device_id={"bead": 2 * ring + (1 - half)},
        device_id_type=MESH,
    )
    moved_copy.start()

    us, vs = [], []
    for e in range(4):
        u, v = [], []
        for blk in range(4):
            row = 4 * (e % 2) + blk
            x = moved[e // 2, row : row + 1]
            y = moved[e // 2, 8 + row : 9 + row]
            z = moved[e // 2, 16 + row : 17 + row]
            u.append(cos_turns(u_q * x - u_off))
            v.append(cos_turns(v_q1 * y + v_q2 * z - v_off))
        us.append(jnp.concatenate(u, axis=1))
        vs.append(jnp.concatenate(v, axis=1))
    raw = lax.dot_general(
        jnp.concatenate(us, axis=0),
        jnp.concatenate(vs, axis=0),
        (((1,), (1,)), ((), ())),
        precision=HIGHEST,
        preferred_element_type=F32,
    )
    raw = jnp.where(same_bead, raw, 0.0)
    by_q = jnp.dot(raw, choose, precision=HIGHEST, preferred_element_type=F32)
    parts = direct * by_q + crossed * pltpu.roll(by_q, 64, 1)
    me = N * half + space
    for e in range(4):
        sum_in[me, e : e + 1] = jnp.sum(parts[8 * e : 8 * e + 8], axis=0, keepdims=True)

    sum_copies = []
    for side in range(2):
        for step in (8, 9, 7, 10, 6, 11, 5, 12, 4, 13, 3, 14, 2, 15, 1, 0):
            if side == 0 and step == 0:
                continue
            copy = pltpu.make_async_remote_copy(
                src_ref=sum_in.at[me],
                dst_ref=sum_in.at[me],
                send_sem=sum_send.at[N * side + step],
                recv_sem=sum_recv.at[N * side + (N - step) % N],
                device_id=plane(side, step),
                device_id_type=MESH,
            )
            copy.start()
            sum_copies.append(copy)
    moved_copy.wait_recv()
    for part, rows in ((half, moved.at[half]), (1 - half, moved_in)):
        for c in range(3):
            for b in range(2):
                for blk in range(4):
                    at = pl.ds(pl.multiple_of(GHOST * part + 128 * blk, 128), 128)
                    row = 8 * c + 4 * b + blk
                    new_pos[c, b : b + 1, at] = rows[row : row + 1, :]
    dense_tiles(1, 3)
    for copy in sum_copies:
        copy.wait_recv()
    total = sum_in[0]
    for r in range(1, 2 * N):
        total = total + sum_in[r]
    all_in[0] = total
    all_copies = []
    for step in (4, 3, 5, 2, 6, 1, 7):
        copy = pltpu.make_async_remote_copy(
            src_ref=all_in.at[0],
            dst_ref=all_in.at[RING - step],
            send_sem=all_send.at[step],
            recv_sem=all_recv.at[RING - step],
            device_id={"bead": 2 * lax.rem(ring + step, RING) + half},
            device_id_type=MESH,
        )
        copy.start()
        all_copies.append(copy)
    dense_tiles(3, 4)
    for copy in all_copies:
        copy.wait_recv()
    every = jnp.concatenate([all_in[r] for r in range(RING)], axis=0)
    for b in range(2):
        own = jnp.where(half == 0, every[b : b + 1], every[2 + b : 3 + b])
        prod = every * (own * (1.0 / (APD * N)))
        prod = prod + pltpu.roll(prod, 64, 1)
        low = prod if b == 0 else jnp.concatenate([prod[b:], prod[0:b]], axis=0)
        high = jnp.concatenate([prod[b + 2 :], prod[0 : b + 2]], axis=0)
        corr[b] = jnp.where(half == 0, low, high)[:, 0:64]

    for copy in small + ghosts + pos_copies + force_copies + [moved_copy] + sum_copies + all_copies:
        copy.wait_send()


def write_out(feats_in, pos_in, corr_in, feats_out, pos_out, corr_out, sems):
    copies = []
    for source, target in ((feats_in, feats_out), (pos_in, pos_out), (corr_in, corr_out)):
        copy = pltpu.make_async_copy(source, target, sems.at[len(copies)])
        copy.start()
        copies.append(copy)
    for copy in copies:
        copy.wait()


def on_device(
    features, positions, send_rows, neighbours, nbr_mask, w_pair, w_in, w_out, omega, q_index
):
    vmem = pl.BlockSpec(memory_space=pltpu.VMEM)
    hbm = pl.BlockSpec(memory_space=pltpu.HBM)
    dma = pltpu.SemaphoreType.DMA
    shapes = (
        jax.ShapeDtypeStruct((2, APD, W), BF16),
        jax.ShapeDtypeStruct((3, 2, APD), F32),
        jax.ShapeDtypeStruct((2, 32, 64), F32),
    )
    results = pl.pallas_call(
        kernel,
        out_shape=shapes,
        in_specs=[hbm] * 10,
        out_specs=(vmem, vmem, vmem),
        scratch_shapes=[
            pltpu.VMEM((2, APD, W), BF16),
            pltpu.VMEM((3, 2, APD), F32),
            pltpu.VMEM((1, 2, GHOST), jnp.int32),
            pltpu.VMEM((SLOTS, APD), jnp.int32),
            pltpu.VMEM((SLOTS, APD), jnp.int32),
            pltpu.VMEM((1, W), BF16),
            pltpu.VMEM((2 * W, 512), BF16),
            pltpu.VMEM((512, W), BF16),
            pltpu.SMEM((2,), F32),
            pltpu.VMEM((3, 64), jnp.int32),
            dma((10,)),
            pltpu.VMEM((8, EXT), F32),
            pltpu.VMEM((2, 8, GHOST), F32),
            pltpu.VMEM((2, 2, GHOST, W), BF16),
            pltpu.VMEM((2, 2, GHOST, W), BF16),
            pltpu.VMEM((APD, 128), F32),
            pltpu.VMEM((2, TILE, EXT), BF16),
            pltpu.VMEM((2, 32, 128), F32),
            pltpu.VMEM((N, 32, 128), F32),
            pltpu.VMEM((2, 24, 128), F32),
            pltpu.VMEM((N, 24, 128), F32),
            pltpu.VMEM((2, 32, 128), F32),
            pltpu.VMEM((128, 1024), F32),
            pltpu.VMEM((2, 24, 128), F32),
            pltpu.VMEM((24, 128), F32),
            pltpu.VMEM((2 * N, 4, 128), F32),
            pltpu.VMEM((RING, 4, 128), F32),
            dma((2,)),
            dma((2,)),
            dma((2,)),
            dma((2,)),
            dma((N,)),
            dma((N,)),
            dma((N,)),
            dma((N,)),
            dma((2,)),
            dma((2 * N,)),
            dma((2 * N,)),
            dma((RING,)),
            dma((RING,)),
        ],
        compiler_params=pltpu.CompilerParams(
            collective_id=0, has_side_effects=True, vmem_limit_bytes=64 * 2**20 - 2**17
        ),
    )(
        features,
        jnp.transpose(positions, (1, 0, 2)),
        send_rows,
        neighbours,
        nbr_mask,
        w_pair.reshape(1, W),
        w_in,
        w_out,
        omega,
        q_index,
    )
    new_features, new_positions, correlation = pl.pallas_call(
        write_out,
        out_shape=shapes,
        in_specs=[vmem] * 3,
        out_specs=(hbm, hbm, hbm),
        scratch_shapes=[dma((3,))],
    )(*results)
    return (new_features, jnp.transpose(new_positions, (1, 0, 2)), correlation)


def solution(mesh):
    in_specs = (
        P("bead", "space", None),
        P("bead", None, "space"),
        P("space", None, None),
        P(None, "space"),
        P(None, "space"),
        P(),
        P(),
        P(),
        P("bead"),
        P(),
    )
    out_specs = (P("bead", "space", None), P("bead", None, "space"), P("bead", None, None))
    return jax.shard_map(
        on_device, mesh=mesh, in_specs=in_specs, out_specs=out_specs, check_vma=False
    )
```

```python
import functools
import math

import jax
import jax.numpy as jnp
from jax import lax
from jax.experimental import pallas as pl
from jax.experimental.pallas import tpu as pltpu
from jax.sharding import PartitionSpec as P

MESH = pl.DeviceIdType.MESH
F32 = jnp.float32
BF16 = jnp.bfloat16
HIGHEST = lax.Precision.HIGHEST
N = 16
RING = 8
APD = 1024
GHOST = 512
EXT = 2048
W = 128
SLOTS = 8
TILE = 256
BOX = 32.0


def other(axis, offset):
    return {axis: lax.rem(lax.axis_index(axis) + offset, N)}


def lane_gather(row, index):
    return jnp.take_along_axis(row, index, axis=1, mode="promise_in_bounds")


def cos_turns(t):
    t = t - jnp.round(t)
    u = (t * t) * (math.pi * math.pi / 4.0)
    m = u * (-0.5 + u * (1.0 / 24 + u * (-1.0 / 720 + u * (1.0 / 40320 - u / 3628800))))
    m = 2.0 * m * (m + 2.0)
    m = 2.0 * m * (m + 2.0)
    return 1.0 + m


def dct_entry(k, bead):
    turns = lax.bitwise_and(k * (2 * bead + 1), 127).astype(F32) * (1.0 / 128.0)
    return jnp.where(k == 0, math.sqrt(1.0 / 32), math.sqrt(2.0 / 32)) * cos_turns(turns)


def kernel(
    feats_hbm,
    pos_hbm,
    send_hbm,
    nbr_hbm,
    mask_hbm,
    w_pair_hbm,
    w_in_hbm,
    w_out_hbm,
    omega_hbm,
    q_hbm,
    feats_hbm_out,
    pos_hbm_out,
    corr_hbm_out,
    feats,
    pos,
    send,
    nbr,
    mask,
    w_pair,
    w_in,
    w_out,
    omega,
    q_index,
    load_sem,
    new_feats,
    new_pos,
    corr,
    store_sem,
    table,
    small_out,
    ghost_out,
    wide_feats,
    picks,
    terms,
    dense,
    pos_out,
    pos_in,
    force_out,
    force_in,
    waves,
    coeff,
    moved,
    moved_in,
    sum_in,
    all_in,
    small_send,
    small_recv,
    ghost_send,
    ghost_recv,
    pos_send,
    pos_recv,
    force_send,
    force_recv,
    moved_sem,
    sum_send,
    sum_recv,
    all_send,
    all_recv,
):
    bead = lax.axis_index("bead")
    space = lax.axis_index("space")
    ring = lax.div(bead, 2)
    half = lax.rem(bead, 2)
    barrier = pltpu.get_barrier_semaphore()

    def plane(side, step):
        return {
            "bead": 2 * ring + lax.rem(half + side, 2),
            "space": lax.rem(space + step, N),
        }

    loads = []
    for source, target in (
        (w_pair_hbm, w_pair),
        (feats_hbm, feats),
        (pos_hbm, pos),
        (send_hbm, send),
        (nbr_hbm, nbr),
        (mask_hbm, mask),
        (omega_hbm, omega),
        (w_in_hbm, w_in),
        (w_out_hbm, w_out),
        (q_hbm, q_index),
    ):
        copy = pltpu.make_async_copy(source, target, load_sem.at[len(loads)])
        copy.start()
        loads.append(copy)

    for step in (1, N - 1) + tuple(range(2, N - 1)):
        pl.semaphore_signal(barrier, inc=1, device_id=plane(0, step), device_id_type=MESH)
    for step in range(N):
        pl.semaphore_signal(barrier, inc=1, device_id=plane(1, step), device_id_type=MESH)
    for step in range(1, RING):
        for side in range(2):
            to = 2 * lax.rem(ring + step, RING) + side
            pl.semaphore_signal(barrier, inc=1, device_id={"bead": to}, device_id_type=MESH)
    partners = (N - 1) + N + 2 * (RING - 1)

    for i in range(4):
        loads[i].wait()
    pair_rows = jnp.broadcast_to(w_pair[...], (16, W))
    for b in range(2):
        strength = lax.dot_general(
            pair_rows, feats[b], (((1,), (1,)), ((), ())), preferred_element_type=F32
        )
        for c in range(3):
            table[4 * b + c : 4 * b + c + 1, 0:APD] = pos[c, b : b + 1]
        table[4 * b + 3 : 4 * b + 4, 0:APD] = strength[0:1]

    for side in range(2):
        for blk in range(4):
            idx = jnp.broadcast_to(send[0, side : side + 1, 128 * blk : 128 * blk + 128], (8, 128))
            hi = lax.shift_right_logical(idx, 7)
            lo = lax.bitwise_and(idx, 127)
            acc = jnp.zeros((8, 128), F32)
            for h in range(8):
                got = lane_gather(table[:, 128 * h : 128 * h + 128], lo)
                acc = jnp.where(hi == h, got, acc)
            small_out[side, :, 128 * blk : 128 * blk + 128] = acc

    for i in range(4, 7):
        loads[i].wait()
    for part in range(2):
        for c in range(3):
            for b in range(2):
                for blk in range(4):
                    at = GHOST * part + 128 * blk
                    row = 8 * c + 4 * b + blk
                    pos_out[part, row : row + 1] = pos[c, b : b + 1, at : at + 128]
    angle = jnp.concatenate([jnp.full((1, 128), omega[b], F32) for b in range(2)], axis=0)
    wave_rows = jnp.concatenate([jnp.cos(angle), jnp.sin(angle), jnp.zeros((4, 128), F32)], axis=0)
    for part in range(2):
        pos_out[part, 24:32] = wave_rows

    pl.semaphore_wait(barrier, partners)

    def to_neighbour(source, target, send_sem, recv_sem, side):
        copy = pltpu.make_async_remote_copy(
            src_ref=source,
            dst_ref=target,
            send_sem=send_sem.at[side],
            recv_sem=recv_sem.at[side],
            device_id=other("space", N - 1 if side == 0 else 1),
            device_id_type=MESH,
        )
        copy.start()
        return copy

    small = []
    for side in range(2):
        start = APD + GHOST if side == 0 else APD
        small.append(
            to_neighbour(
                small_out.at[side], table.at[:, pl.ds(start, GHOST)], small_send, small_recv, side
            )
        )

    def to_beads(source, target, send_sem, recv_sem, offsets):
        copies = []
        for o in offsets:
            to = lax.rem(bead + o, N)
            copy = pltpu.make_async_remote_copy(
                src_ref=source.at[lax.rem(to, 2)],
                dst_ref=target.at[bead],
                send_sem=send_sem.at[o],
                recv_sem=recv_sem.at[N - o],
                device_id={"bead": to},
                device_id_type=MESH,
            )
            copy.start()
            copies.append(copy)
        return copies

    crossing = (7, 9, 5, 11, 3, 13, 1, 15)
    straight = (8, 6, 10, 4, 12, 2, 14)
    pos_copies = to_beads(pos_out, pos_in, pos_send, pos_recv, crossing + straight)
    pos_in[bead] = pos_out[half]

    for b in range(2):
        for blk in range(APD // 128):
            at = slice(128 * blk, 128 * blk + 128)
            wide_feats[W * b : W * b + W, at] = jnp.transpose(feats[b, at, :])
    tall = lax.broadcasted_iota(jnp.int32, (APD, GHOST), 0)
    ghosts = []
    for side in range(2):
        hot = (tall == send[0, side : side + 1, :]).astype(F32).astype(BF16)
        ghost_out[side] = jnp.dot(
            wide_feats[:, 0:APD], hot, preferred_element_type=F32
        ).astype(BF16)
        start = APD + GHOST if side == 0 else APD
        ghosts.append(
            to_neighbour(
                ghost_out.at[side],
                wide_feats.at[:, pl.ds(start, GHOST)],
                ghost_send,
                ghost_recv,
                side,
            )
        )

    def pick(at, picked, first, last):
        idx = nbr[:, at]
        hi = lax.shift_right_logical(idx, 7)
        lo = lax.bitwise_and(idx, 127)
        for h in range(first, last):
            hit = hi == h
            for q in range(8):
                row = jnp.broadcast_to(table[q : q + 1, 128 * h : 128 * h + 128], (8, 128))
                picked[q] = jnp.where(hit, lane_gather(row, lo), picked[q])
        return picked

    def own_block(blk, _):
        at = pl.ds(pl.multiple_of(128 * blk, 128), 128)
        got = pick(at, [jnp.zeros((8, 128), F32) for _ in range(8)], 0, APD // 128)
        for q in range(8):
            picks[q, :, at] = got[q]
        return 0

    lax.fori_loop(0, APD // 128, own_block, 0)

    for copy in small:
        copy.wait_recv()

    def block(part, blk):
        at = pl.ds(pl.multiple_of(GHOST * part + 128 * blk, 128), 128)
        picked = pick(at, [picks[q, :, at] for q in range(8)], APD // 128, EXT // 128)
        idx = nbr[:, at]
        live = mask[:, at].astype(F32)
        hi = lax.shift_right_logical(idx, 7)
        lo = lax.bitwise_and(idx, 127)
        code = (128 + lo).astype(F32) * lax.shift_left(jnp.ones_like(hi), hi).astype(F32)
        cs = []
        for b in range(2):
            d = []
            for c in range(3):
                d.append(table[4 * b + c : 4 * b + c + 1, at] - picked[4 * b + c])
            first = d[0]
            d[0] = jnp.where(
                first > BOX / 2,
                first - BOX,
                jnp.where(first < -BOX / 2, first + BOX, first),
            )
            dist = d[0] * d[0] + d[1] * d[1] + d[2] * d[2]
            weight = live / (1.0 + dist / 4.0)
            pair = weight * (table[4 * b + 3 : 4 * b + 4, at] + picked[4 * b + 3])
            for c in range(3):
                row = pl.ds(8 * c + 4 * b + blk, 1)
                force_out[part, row, :] = jnp.sum(pair * d[c], axis=0, keepdims=True)
            cs.append(weight)
        total = list(cs)
        for r in range(1, SLOTS):
            same = pltpu.roll(idx, r, 0) == idx
            for b in range(2):
                total[b] = total[b] + jnp.where(same, pltpu.roll(cs[b], r, 0), 0.0)
        terms[0, :, at] = code
        terms[1, :, at] = total[0]
        terms[2, :, at] = total[1]

    def blocks(part):
        def step(blk, _):
            block(part, blk)
            return 0

        lax.fori_loop(0, 4, step, 0)

    blocks(1 - half)
    force_copies = to_beads(force_out, force_in, force_send, force_recv, crossing)
    blocks(half)
    force_copies += to_beads(force_out, force_in, force_send, force_recv, straight)
    force_in[bead] = force_out[half]

    for copy in pos_copies:
        copy.wait_recv()
    for source in range(N):
        waves[0, 2 * source : 2 * source + 2] = pos_in[source, 24:26]
        waves[1, 2 * source : 2 * source + 2] = pos_in[source, 26:28]
    k_rows = lax.broadcasted_iota(jnp.int32, (32, 128), 0)
    by_mode = []
    for e in range(4):
        entry = dct_entry(k_rows, 4 * ring + e)
        by_mode += [entry * waves[0], entry * waves[1]]
    rows = lax.broadcasted_iota(jnp.int32, (128, 32), 0)
    source_bead = 2 * lax.shift_right_logical(rows, 3) + lax.bitwise_and(
        lax.shift_right_logical(rows, 2), 1
    )
    spread = dct_entry(lax.broadcasted_iota(jnp.int32, (128, 32), 1), source_bead)
    coeff[...] = jnp.dot(
        spread,
        jnp.concatenate(by_mode, axis=1),
        precision=HIGHEST,
        preferred_element_type=F32,
    )

    def mix(kind, data, acc):
        for source in range(N):
            for c in range(3):
                value = data[source, 8 * c : 8 * c + 8]
                for e in range(4):
                    lanes = slice(128 * (2 * e + kind), 128 * (2 * e + kind) + 128)
                    acc[3 * e + c] = acc[3 * e + c] + coeff[8 * source : 8 * source + 8, lanes] * value
        return acc

    acc = mix(0, pos_in, [jnp.zeros((8, 128), F32) for _ in range(12)])

    for i in range(7, 10):
        loads[i].wait()
    for copy in ghosts:
        copy.wait_recv()

    sub_code = (128 + lax.broadcasted_iota(jnp.int32, (16, 128), 0)).astype(F32)

    def dense_tile(t):
        for blk in range(TILE // 128):
            lanes = slice(128 * blk, 128 * blk + 128)
            at = pl.ds(pl.multiple_of(t * TILE + 128 * blk, 128), 128)

            def spread_row(kind, k):
                return jnp.broadcast_to(terms[kind, k : k + 1, at], (16, 128)).astype(BF16)

            codes, c0, c1 = [[spread_row(kind, k) for k in range(SLOTS)] for kind in range(3)]

            def strip(s, _):
                base = sub_code + (16 * s).astype(F32)
                for h in range(EXT // 128):
                    here = (base * float(2**h)).astype(BF16)
                    a0 = jnp.zeros((16, 128), BF16)
                    a1 = jnp.zeros((16, 128), BF16)
                    for k in range(SLOTS):
                        hit = codes[k] == here
                        a0 = jnp.where(hit, c0[k], a0)
                        a1 = jnp.where(hit, c1[k], a1)
                    row = pl.ds(pl.multiple_of(128 * h + 16 * s, 16), 16)
                    dense[0, row, lanes] = a0
                    dense[1, row, lanes] = a1
                return 0

            lax.fori_loop(0, 8, strip, 0)
        at = pl.ds(pl.multiple_of(t * TILE, TILE), TILE)
        for b in range(2):
            agg = jnp.dot(wide_feats[W * b : W * b + W], dense[b], preferred_element_type=F32)
            agg = jnp.transpose(agg)
            mine = feats[b, at, :]
            joined = jnp.concatenate([mine, agg.astype(BF16)], axis=1)
            x = jnp.dot(joined, w_in[...], preferred_element_type=F32)
            hidden = (x * (0.5 * (1.0 + jnp.tanh(0.5 * x)))).astype(BF16)
            out = mine.astype(F32) + jnp.dot(hidden, w_out[...], preferred_element_type=F32)
            new_feats[b, at, :] = out.astype(BF16)

    def dense_tiles(first, last):
        def step(t, _):
            dense_tile(t)
            return 0

        lax.fori_loop(first, last, step, 0)

    stores = []

    def store(source, target):
        copy = pltpu.make_async_copy(source, target, store_sem.at[len(stores)])
        copy.start()
        stores.append(copy)

    def dense_rows(first, last):
        dense_tiles(first, last)
        for b in range(2):
            rows = pl.ds(first * TILE, (last - first) * TILE)
            store(new_feats.at[b, rows], feats_hbm_out.at[b, rows])

    dense_rows(0, 2)

    q0 = q_index[0:1, :]
    pick = 4 * (q_index[1:2, :] - 1) + (q_index[2:3, :] - 1)
    pick = jnp.concatenate([pick, pick + 16], axis=1)
    q0 = jnp.concatenate([q0, q0], axis=1)
    row128 = lax.broadcasted_iota(jnp.int32, (128, 128), 0)
    choose = (lax.bitwise_and(row128, 31) == pick).astype(F32)
    row32 = lax.broadcasted_iota(jnp.int32, (32, 128), 0)
    lane32 = lax.broadcasted_iota(jnp.int32, (32, 128), 1)
    row8 = lax.bitwise_and(row32, 7)
    direct = (row8 == q0 - 1).astype(F32)
    crossed = jnp.where(row8 == q0 + 3, jnp.where(lane32 < 64, -1.0, 1.0), 0.0)
    same_bead = lax.shift_right_logical(row32, 3) == lax.shift_right_logical(lane32, 5)
    r8 = lax.broadcasted_iota(jnp.int32, (8, 128), 0)
    u_q = (lax.bitwise_and(r8, 3) + 1).astype(F32) * (1.0 / BOX)
    u_off = jnp.where(r8 >= 4, 0.25, 0.0)
    v_q1 = (lax.bitwise_and(lax.shift_right_logical(row32, 2), 3) + 1).astype(F32) * 0.25
    v_q2 = (lax.bitwise_and(row32, 3) + 1).astype(F32) * 0.25
    v_off = jnp.where(row32 >= 16, 0.25, 0.0)

    for copy in force_copies:
        copy.wait_recv()
    acc = mix(1, force_in, acc)
    for e in range(4):
        for c in range(3):
            row = 8 * c + 4 * (e % 2)
            value = acc[3 * e + c]
            moved[e // 2, row : row + 4] = (value + pltpu.roll(value, 4, 0))[0:4]
    moved_copy = pltpu.make_async_remote_copy(
        src_ref=moved.at[1 - half],
        dst_ref=moved_in,
        send_sem=moved_sem.at[0],
        recv_sem=moved_sem.at[1],
        device_id={"bead": 2 * ring + (1 - half)},
        device_id_type=MESH,
    )
    moved_copy.start()

    us, vs = [], []
    for e in range(4):
        u, v = [], []
        for blk in range(4):
            row = 4 * (e % 2) + blk
            x = moved[e // 2, row : row + 1]
            y = moved[e // 2, 8 + row : 9 + row]
            z = moved[e // 2, 16 + row : 17 + row]
            u.append(cos_turns(u_q * x - u_off))
            v.append(cos_turns(v_q1 * y + v_q2 * z - v_off))
        us.append(jnp.concatenate(u, axis=1))
        vs.append(jnp.concatenate(v, axis=1))
    raw = lax.dot_general(
        jnp.concatenate(us, axis=0),
        jnp.concatenate(vs, axis=0),
        (((1,), (1,)), ((), ())),
        precision=HIGHEST,
        preferred_element_type=F32,
    )
    raw = jnp.where(same_bead, raw, 0.0)
    by_q = jnp.dot(raw, choose, precision=HIGHEST, preferred_element_type=F32)
    parts = direct * by_q + crossed * pltpu.roll(by_q, 64, 1)
    me = N * half + space
    for e in range(4):
        sum_in[me, e : e + 1] = jnp.sum(parts[8 * e : 8 * e + 8], axis=0, keepdims=True)

    sum_copies = []
    for side in range(2):
        for step in (8, 9, 7, 10, 6, 11, 5, 12, 4, 13, 3, 14, 2, 15, 1, 0):
            if side == 0 and step == 0:
                continue
            copy = pltpu.make_async_remote_copy(
                src_ref=sum_in.at[me],
                dst_ref=sum_in.at[me],
                send_sem=sum_send.at[N * side + step],
                recv_sem=sum_recv.at[N * side + (N - step) % N],
                device_id=plane(side, step),
                device_id_type=MESH,
            )
            copy.start()
            sum_copies.append(copy)
    moved_copy.wait_recv()
    for part, rows in ((half, moved.at[half]), (1 - half, moved_in)):
        for c in range(3):
            for b in range(2):
                for blk in range(4):
                    at = pl.ds(pl.multiple_of(GHOST * part + 128 * blk, 128), 128)
                    row = 8 * c + 4 * b + blk
                    new_pos[c, b : b + 1, at] = rows[row : row + 1, :]
    store(new_pos, pos_hbm_out)
    dense_rows(2, 3)
    for copy in sum_copies:
        copy.wait_recv()
    total = sum_in[0]
    for r in range(1, 2 * N):
        total = total + sum_in[r]
    all_in[0] = total
    all_copies = []
    for step in (4, 3, 5, 2, 6, 1, 7):
        copy = pltpu.make_async_remote_copy(
            src_ref=all_in.at[0],
            dst_ref=all_in.at[RING - step],
            send_sem=all_send.at[step],
            recv_sem=all_recv.at[RING - step],
            device_id={"bead": 2 * lax.rem(ring + step, RING) + half},
            device_id_type=MESH,
        )
        copy.start()
        all_copies.append(copy)
    dense_rows(3, 4)
    for copy in all_copies:
        copy.wait_recv()
    every = jnp.concatenate([all_in[r] for r in range(RING)], axis=0)
    for b in range(2):
        own = jnp.where(half == 0, every[b : b + 1], every[2 + b : 3 + b])
        prod = every * (own * (1.0 / (APD * N)))
        prod = prod + pltpu.roll(prod, 64, 1)
        low = prod if b == 0 else jnp.concatenate([prod[b:], prod[0:b]], axis=0)
        high = jnp.concatenate([prod[b + 2 :], prod[0 : b + 2]], axis=0)
        corr[b] = jnp.where(half == 0, low, high)[:, 0:64]

    store(corr, corr_hbm_out)
    for copy in small + ghosts + pos_copies + force_copies + [moved_copy] + sum_copies + all_copies:
        copy.wait_send()
    for copy in stores:
        copy.wait()


def write_out(feats_in, pos_in, corr_in, feats_out, pos_out, corr_out, sems):
    copies = []
    for source, target in ((feats_in, feats_out), (pos_in, pos_out), (corr_in, corr_out)):
        copy = pltpu.make_async_copy(source, target, sems.at[len(copies)])
        copy.start()
        copies.append(copy)
    for copy in copies:
        copy.wait()


def on_device(
    features, positions, send_rows, neighbours, nbr_mask, w_pair, w_in, w_out, omega, q_index
):
    hbm = pl.BlockSpec(memory_space=pltpu.HBM)
    dma = pltpu.SemaphoreType.DMA
    shapes = (
        jax.ShapeDtypeStruct((2, APD, W), BF16),
        jax.ShapeDtypeStruct((3, 2, APD), F32),
        jax.ShapeDtypeStruct((2, 32, 64), F32),
    )
    results = pl.pallas_call(
        kernel,
        out_shape=shapes,
        in_specs=[hbm] * 10,
        out_specs=(hbm, hbm, hbm),
        scratch_shapes=[
            pltpu.VMEM((2, APD, W), BF16),
            pltpu.VMEM((3, 2, APD), F32),
            pltpu.VMEM((1, 2, GHOST), jnp.int32),
            pltpu.VMEM((SLOTS, APD), jnp.int32),
            pltpu.VMEM((SLOTS, APD), jnp.int32),
            pltpu.VMEM((1, W), BF16),
            pltpu.VMEM((2 * W, 512), BF16),
            pltpu.VMEM((512, W), BF16),
            pltpu.SMEM((2,), F32),
            pltpu.VMEM((3, 64), jnp.int32),
            dma((10,)),
            pltpu.VMEM((2, APD, W), BF16),
            pltpu.VMEM((3, 2, APD), F32),
            pltpu.VMEM((2, 32, 64), F32),
            dma((8,)),
            pltpu.VMEM((8, EXT), F32),
            pltpu.VMEM((2, 8, GHOST), F32),
            pltpu.VMEM((2, 2 * W, GHOST), BF16),
            pltpu.VMEM((2 * W, EXT), BF16),
            pltpu.VMEM((8, SLOTS, APD), F32),
            pltpu.VMEM((3, SLOTS, APD), F32),
            pltpu.VMEM((2, EXT, TILE), BF16),
            pltpu.VMEM((2, 32, 128), F32),
            pltpu.VMEM((N, 32, 128), F32),
            pltpu.VMEM((2, 24, 128), F32),
            pltpu.VMEM((N, 24, 128), F32),
            pltpu.VMEM((2, 32, 128), F32),
            pltpu.VMEM((128, 1024), F32),
            pltpu.VMEM((2, 24, 128), F32),
            pltpu.VMEM((24, 128), F32),
            pltpu.VMEM((2 * N, 4, 128), F32),
            pltpu.VMEM((RING, 4, 128), F32),
            dma((2,)),
            dma((2,)),
            dma((2,)),
            dma((2,)),
            dma((N,)),
            dma((N,)),
            dma((N,)),
            dma((N,)),
            dma((2,)),
            dma((2 * N,)),
            dma((2 * N,)),
            dma((RING,)),
            dma((RING,)),
        ],
        compiler_params=pltpu.CompilerParams(
            collective_id=0, has_side_effects=True, vmem_limit_bytes=64 * 2**20 - 2**17
        ),
    )(
        features,
        jnp.transpose(positions, (1, 0, 2)),
        send_rows,
        neighbours,
        nbr_mask,
        w_pair.reshape(1, W),
        w_in,
        w_out,
        omega,
        q_index,
    )
    new_features, new_positions, correlation = pl.pallas_call(
        write_out,
        out_shape=shapes,
        in_specs=[pl.BlockSpec(memory_space=pltpu.VMEM)] * 3,
        out_specs=(hbm, hbm, hbm),
        scratch_shapes=[dma((3,))],
    )(*results)
    return (new_features, jnp.transpose(new_positions, (1, 0, 2)), correlation)


def solution(mesh):
    in_specs = (
        P("bead", "space", None),
        P("bead", None, "space"),
        P("space", None, None),
        P(None, "space"),
        P(None, "space"),
        P(),
        P(),
        P(),
        P("bead"),
        P(),
    )
    out_specs = (P("bead", "space", None), P("bead", None, "space"), P("bead", None, None))
    return jax.shard_map(
        on_device, mesh=mesh, in_specs=in_specs, out_specs=out_specs, check_vma=False
    )
```

```python
import functools
import math

import jax
import jax.numpy as jnp
from jax import lax
from jax.experimental import pallas as pl
from jax.experimental.pallas import tpu as pltpu
from jax.sharding import PartitionSpec as P

MESH = pl.DeviceIdType.MESH
F32 = jnp.float32
BF16 = jnp.bfloat16
HIGHEST = lax.Precision.HIGHEST
N = 16
RING = 8
APD = 1024
GHOST = 512
EXT = 2048
W = 128
SLOTS = 8
TILE = 256
BOX = 32.0


def other(axis, offset):
    return {axis: lax.rem(lax.axis_index(axis) + offset, N)}


def lane_gather(row, index):
    return jnp.take_along_axis(row, index, axis=1, mode="promise_in_bounds")


def cos_turns(t):
    t = t - jnp.round(t)
    u = (t * t) * (math.pi * math.pi / 4.0)
    m = u * (-0.5 + u * (1.0 / 24 + u * (-1.0 / 720 + u * (1.0 / 40320 - u / 3628800))))
    m = 2.0 * m * (m + 2.0)
    m = 2.0 * m * (m + 2.0)
    return 1.0 + m


def dct_entry(k, bead):
    turns = lax.bitwise_and(k * (2 * bead + 1), 127).astype(F32) * (1.0 / 128.0)
    return jnp.where(k == 0, math.sqrt(1.0 / 32), math.sqrt(2.0 / 32)) * cos_turns(turns)


def kernel(
    feats_hbm,
    pos_hbm,
    send_hbm,
    nbr_hbm,
    mask_hbm,
    w_pair_hbm,
    w_in_hbm,
    w_out_hbm,
    omega_hbm,
    q_hbm,
    feats_hbm_out,
    pos_hbm_out,
    corr_hbm_out,
    feats,
    pos,
    send,
    nbr,
    mask,
    w_pair,
    w_in,
    w_out,
    omega,
    q_index,
    load_sem,
    new_feats,
    new_pos,
    corr,
    store_sem,
    table,
    small_out,
    ghost_out,
    wide_feats,
    picks,
    terms,
    agg_own,
    dense,
    pos_out,
    pos_in,
    force_out,
    force_in,
    waves,
    coeff,
    moved,
    moved_in,
    sum_in,
    all_in,
    small_send,
    small_recv,
    ghost_send,
    ghost_recv,
    pos_send,
    pos_recv,
    force_send,
    force_recv,
    moved_sem,
    sum_send,
    sum_recv,
    all_send,
    all_recv,
):
    bead = lax.axis_index("bead")
    space = lax.axis_index("space")
    ring = lax.div(bead, 2)
    half = lax.rem(bead, 2)
    barrier = pltpu.get_barrier_semaphore()

    def plane(side, step):
        return {
            "bead": 2 * ring + lax.rem(half + side, 2),
            "space": lax.rem(space + step, N),
        }

    loads = []
    for source, target in (
        (w_pair_hbm, w_pair),
        (feats_hbm, feats),
        (pos_hbm, pos),
        (send_hbm, send),
        (nbr_hbm, nbr),
        (mask_hbm, mask),
        (omega_hbm, omega),
        (w_in_hbm, w_in),
        (w_out_hbm, w_out),
        (q_hbm, q_index),
    ):
        copy = pltpu.make_async_copy(source, target, load_sem.at[len(loads)])
        copy.start()
        loads.append(copy)

    for step in (1, N - 1) + tuple(range(2, N - 1)):
        pl.semaphore_signal(barrier, inc=1, device_id=plane(0, step), device_id_type=MESH)
    for step in range(N):
        pl.semaphore_signal(barrier, inc=1, device_id=plane(1, step), device_id_type=MESH)
    for step in range(1, RING):
        for side in range(2):
            to = 2 * lax.rem(ring + step, RING) + side
            pl.semaphore_signal(barrier, inc=1, device_id={"bead": to}, device_id_type=MESH)
    partners = (N - 1) + N + 2 * (RING - 1)

    for i in range(4):
        loads[i].wait()
    pair_rows = jnp.broadcast_to(w_pair[...], (16, W))
    for b in range(2):
        strength = lax.dot_general(
            pair_rows, feats[b], (((1,), (1,)), ((), ())), preferred_element_type=F32
        )
        for c in range(3):
            table[4 * b + c : 4 * b + c + 1, 0:APD] = pos[c, b : b + 1]
        table[4 * b + 3 : 4 * b + 4, 0:APD] = strength[0:1]

    for side in range(2):
        for blk in range(4):
            idx = jnp.broadcast_to(send[0, side : side + 1, 128 * blk : 128 * blk + 128], (8, 128))
            hi = lax.shift_right_logical(idx, 7)
            lo = lax.bitwise_and(idx, 127)
            acc = jnp.zeros((8, 128), F32)
            for h in range(8):
                got = lane_gather(table[:, 128 * h : 128 * h + 128], lo)
                acc = jnp.where(hi == h, got, acc)
            small_out[side, :, 128 * blk : 128 * blk + 128] = acc

    for i in range(4, 7):
        loads[i].wait()
    for part in range(2):
        for c in range(3):
            for b in range(2):
                for blk in range(4):
                    at = GHOST * part + 128 * blk
                    row = 8 * c + 4 * b + blk
                    pos_out[part, row : row + 1] = pos[c, b : b + 1, at : at + 128]
    angle = jnp.concatenate([jnp.full((1, 128), omega[b], F32) for b in range(2)], axis=0)
    wave_rows = jnp.concatenate([jnp.cos(angle), jnp.sin(angle), jnp.zeros((4, 128), F32)], axis=0)
    for part in range(2):
        pos_out[part, 24:32] = wave_rows

    pl.semaphore_wait(barrier, partners)

    def to_neighbour(source, target, send_sem, recv_sem, side):
        copy = pltpu.make_async_remote_copy(
            src_ref=source,
            dst_ref=target,
            send_sem=send_sem.at[side],
            recv_sem=recv_sem.at[side],
            device_id=other("space", N - 1 if side == 0 else 1),
            device_id_type=MESH,
        )
        copy.start()
        return copy

    small = []
    for side in range(2):
        start = APD + GHOST if side == 0 else APD
        small.append(
            to_neighbour(
                small_out.at[side], table.at[:, pl.ds(start, GHOST)], small_send, small_recv, side
            )
        )

    def to_beads(source, target, send_sem, recv_sem, offsets):
        copies = []
        for o in offsets:
            to = lax.rem(bead + o, N)
            copy = pltpu.make_async_remote_copy(
                src_ref=source.at[lax.rem(to, 2)],
                dst_ref=target.at[bead],
                send_sem=send_sem.at[o],
                recv_sem=recv_sem.at[N - o],
                device_id={"bead": to},
                device_id_type=MESH,
            )
            copy.start()
            copies.append(copy)
        return copies

    crossing = (7, 9, 5, 11, 3, 13, 1, 15)
    straight = (8, 6, 10, 4, 12, 2, 14)
    pos_copies = to_beads(pos_out, pos_in, pos_send, pos_recv, crossing + straight)
    pos_in[bead] = pos_out[half]

    for b in range(2):
        for blk in range(APD // 128):
            at = slice(128 * blk, 128 * blk + 128)
            wide_feats[W * b : W * b + W, at] = jnp.transpose(feats[b, at, :])
    tall = lax.broadcasted_iota(jnp.int32, (APD, GHOST), 0)
    for side in range(2):
        hot = (tall == send[0, side : side + 1, :]).astype(F32).astype(BF16)
        ghost_out[side] = jnp.dot(
            wide_feats[:, 0:APD], hot, preferred_element_type=F32
        ).astype(BF16)

    def pick(at, picked, first, last):
        idx = nbr[:, at]
        hi = lax.shift_right_logical(idx, 7)
        lo = lax.bitwise_and(idx, 127)
        for h in range(first, last):
            hit = hi == h
            for q in range(8):
                row = jnp.broadcast_to(table[q : q + 1, 128 * h : 128 * h + 128], (8, 128))
                picked[q] = jnp.where(hit, lane_gather(row, lo), picked[q])
        return picked

    def own_block(blk, _):
        at = pl.ds(pl.multiple_of(128 * blk, 128), 128)
        got = pick(at, [jnp.zeros((8, 128), F32) for _ in range(8)], 0, APD // 128)
        for q in range(8):
            picks[q, :, at] = got[q]
        return 0

    lax.fori_loop(0, APD // 128, own_block, 0)

    for copy in small:
        copy.wait_recv()

    def block(part, blk):
        at = pl.ds(pl.multiple_of(GHOST * part + 128 * blk, 128), 128)
        picked = pick(at, [picks[q, :, at] for q in range(8)], APD // 128, EXT // 128)
        idx = nbr[:, at]
        live = mask[:, at].astype(F32)
        hi = lax.shift_right_logical(idx, 7)
        lo = lax.bitwise_and(idx, 127)
        code = (128 + lo).astype(F32) * lax.shift_left(jnp.ones_like(hi), hi).astype(F32)
        cs = []
        for b in range(2):
            d = []
            for c in range(3):
                d.append(table[4 * b + c : 4 * b + c + 1, at] - picked[4 * b + c])
            first = d[0]
            d[0] = jnp.where(
                first > BOX / 2,
                first - BOX,
                jnp.where(first < -BOX / 2, first + BOX, first),
            )
            dist = d[0] * d[0] + d[1] * d[1] + d[2] * d[2]
            weight = live / (1.0 + dist / 4.0)
            pair = weight * (table[4 * b + 3 : 4 * b + 4, at] + picked[4 * b + 3])
            for c in range(3):
                row = pl.ds(8 * c + 4 * b + blk, 1)
                force_out[part, row, :] = jnp.sum(pair * d[c], axis=0, keepdims=True)
            cs.append(weight)
        total = list(cs)
        for r in range(1, SLOTS):
            same = pltpu.roll(idx, r, 0) == idx
            for b in range(2):
                total[b] = total[b] + jnp.where(same, pltpu.roll(cs[b], r, 0), 0.0)
        terms[0, :, at] = code
        terms[1, :, at] = total[0]
        terms[2, :, at] = total[1]

    def blocks(part):
        def step(blk, _):
            block(part, blk)
            return 0

        lax.fori_loop(0, 4, step, 0)

    blocks(1 - half)
    force_copies = to_beads(force_out, force_in, force_send, force_recv, crossing)
    blocks(half)
    force_copies += to_beads(force_out, force_in, force_send, force_recv, straight)
    force_in[bead] = force_out[half]
    ghosts = []
    for side in range(2):
        start = APD + GHOST if side == 0 else APD
        ghosts.append(
            to_neighbour(
                ghost_out.at[side],
                wide_feats.at[:, pl.ds(start, GHOST)],
                ghost_send,
                ghost_recv,
                side,
            )
        )

    sub_code = (128 + lax.broadcasted_iota(jnp.int32, (16, 128), 0)).astype(F32)

    def dense_half(t, first):
        for blk in range(TILE // 128):
            lanes = slice(128 * blk, 128 * blk + 128)
            at = pl.ds(pl.multiple_of(t * TILE + 128 * blk, 128), 128)

            def spread_row(kind, k):
                return jnp.broadcast_to(terms[kind, k : k + 1, at], (16, 128)).astype(BF16)

            codes, c0, c1 = [[spread_row(kind, k) for k in range(SLOTS)] for kind in range(3)]

            def strip(s, _):
                base = sub_code + (16 * s).astype(F32)
                for h in range(8):
                    here = (base * float(2 ** (first // 128 + h))).astype(BF16)
                    a0 = jnp.zeros((16, 128), BF16)
                    a1 = jnp.zeros((16, 128), BF16)
                    for k in range(SLOTS):
                        hit = codes[k] == here
                        a0 = jnp.where(hit, c0[k], a0)
                        a1 = jnp.where(hit, c1[k], a1)
                    row = pl.ds(pl.multiple_of(128 * h + 16 * s, 16), 16)
                    dense[0, row, lanes] = a0
                    dense[1, row, lanes] = a1
                return 0

            lax.fori_loop(0, 8, strip, 0)
        return [
            jnp.dot(
                wide_feats[W * b : W * b + W, first : first + APD],
                dense[b],
                preferred_element_type=F32,
            )
            for b in range(2)
        ]

    def own_tile(t, _):
        at = pl.ds(pl.multiple_of(t * TILE, TILE), TILE)
        agg_own[0, :, at], agg_own[1, :, at] = dense_half(t, 0)
        return 0

    def dense_tile(t):
        at = pl.ds(pl.multiple_of(t * TILE, TILE), TILE)
        ghost_part = dense_half(t, APD)
        for b in range(2):
            agg = jnp.transpose(agg_own[b, :, at] + ghost_part[b])
            mine = feats[b, at, :]
            joined = jnp.concatenate([mine, agg.astype(BF16)], axis=1)
            x = jnp.dot(joined, w_in[...], preferred_element_type=F32)
            hidden = (x * (0.5 * (1.0 + jnp.tanh(0.5 * x)))).astype(BF16)
            out = mine.astype(F32) + jnp.dot(hidden, w_out[...], preferred_element_type=F32)
            new_feats[b, at, :] = out.astype(BF16)

    def dense_tiles(first, last):
        def step(t, _):
            dense_tile(t)
            return 0

        lax.fori_loop(first, last, step, 0)

    stores = []

    def store(source, target):
        copy = pltpu.make_async_copy(source, target, store_sem.at[len(stores)])
        copy.start()
        stores.append(copy)

    def dense_rows(first, last):
        dense_tiles(first, last)
        for b in range(2):
            rows = pl.ds(first * TILE, (last - first) * TILE)
            store(new_feats.at[b, rows], feats_hbm_out.at[b, rows])

    lax.fori_loop(0, APD // TILE, own_tile, 0)

    for copy in pos_copies:
        copy.wait_recv()
    for source in range(N):
        waves[0, 2 * source : 2 * source + 2] = pos_in[source, 24:26]
        waves[1, 2 * source : 2 * source + 2] = pos_in[source, 26:28]
    k_rows = lax.broadcasted_iota(jnp.int32, (32, 128), 0)
    by_mode = []
    for e in range(4):
        entry = dct_entry(k_rows, 4 * ring + e)
        by_mode += [entry * waves[0], entry * waves[1]]
    rows = lax.broadcasted_iota(jnp.int32, (128, 32), 0)
    source_bead = 2 * lax.shift_right_logical(rows, 3) + lax.bitwise_and(
        lax.shift_right_logical(rows, 2), 1
    )
    spread = dct_entry(lax.broadcasted_iota(jnp.int32, (128, 32), 1), source_bead)
    coeff[...] = jnp.dot(
        spread,
        jnp.concatenate(by_mode, axis=1),
        precision=HIGHEST,
        preferred_element_type=F32,
    )

    def mix(kind, data, acc):
        for source in range(N):
            for c in range(3):
                value = data[source, 8 * c : 8 * c + 8]
                for e in range(4):
                    lanes = slice(128 * (2 * e + kind), 128 * (2 * e + kind) + 128)
                    acc[3 * e + c] = acc[3 * e + c] + coeff[8 * source : 8 * source + 8, lanes] * value
        return acc

    acc = mix(0, pos_in, [jnp.zeros((8, 128), F32) for _ in range(12)])

    for i in range(7, 10):
        loads[i].wait()
    for copy in ghosts:
        copy.wait_recv()

    q0 = q_index[0:1, :]
    pick = 4 * (q_index[1:2, :] - 1) + (q_index[2:3, :] - 1)
    pick = jnp.concatenate([pick, pick + 16], axis=1)
    q0 = jnp.concatenate([q0, q0], axis=1)
    row128 = lax.broadcasted_iota(jnp.int32, (128, 128), 0)
    choose = (lax.bitwise_and(row128, 31) == pick).astype(F32)
    row32 = lax.broadcasted_iota(jnp.int32, (32, 128), 0)
    lane32 = lax.broadcasted_iota(jnp.int32, (32, 128), 1)
    row8 = lax.bitwise_and(row32, 7)
    direct = (row8 == q0 - 1).astype(F32)
    crossed = jnp.where(row8 == q0 + 3, jnp.where(lane32 < 64, -1.0, 1.0), 0.0)
    same_bead = lax.shift_right_logical(row32, 3) == lax.shift_right_logical(lane32, 5)
    r8 = lax.broadcasted_iota(jnp.int32, (8, 128), 0)
    u_q = (lax.bitwise_and(r8, 3) + 1).astype(F32) * (1.0 / BOX)
    u_off = jnp.where(r8 >= 4, 0.25, 0.0)
    v_q1 = (lax.bitwise_and(lax.shift_right_logical(row32, 2), 3) + 1).astype(F32) * 0.25
    v_q2 = (lax.bitwise_and(row32, 3) + 1).astype(F32) * 0.25
    v_off = jnp.where(row32 >= 16, 0.25, 0.0)

    for copy in force_copies:
        copy.wait_recv()
    acc = mix(1, force_in, acc)
    for e in range(4):
        for c in range(3):
            row = 8 * c + 4 * (e % 2)
            value = acc[3 * e + c]
            moved[e // 2, row : row + 4] = (value + pltpu.roll(value, 4, 0))[0:4]
    moved_copy = pltpu.make_async_remote_copy(
        src_ref=moved.at[1 - half],
        dst_ref=moved_in,
        send_sem=moved_sem.at[0],
        recv_sem=moved_sem.at[1],
        device_id={"bead": 2 * ring + (1 - half)},
        device_id_type=MESH,
    )
    moved_copy.start()

    us, vs = [], []
    for e in range(4):
        u, v = [], []
        for blk in range(4):
            row = 4 * (e % 2) + blk
            x = moved[e // 2, row : row + 1]
            y = moved[e // 2, 8 + row : 9 + row]
            z = moved[e // 2, 16 + row : 17 + row]
            u.append(cos_turns(u_q * x - u_off))
            v.append(cos_turns(v_q1 * y + v_q2 * z - v_off))
        us.append(jnp.concatenate(u, axis=1))
        vs.append(jnp.concatenate(v, axis=1))
    raw = lax.dot_general(
        jnp.concatenate(us, axis=0),
        jnp.concatenate(vs, axis=0),
        (((1,), (1,)), ((), ())),
        precision=HIGHEST,
        preferred_element_type=F32,
    )
    raw = jnp.where(same_bead, raw, 0.0)
    by_q = jnp.dot(raw, choose, precision=HIGHEST, preferred_element_type=F32)
    parts = direct * by_q + crossed * pltpu.roll(by_q, 64, 1)
    me = N * half + space
    for e in range(4):
        sum_in[me, e : e + 1] = jnp.sum(parts[8 * e : 8 * e + 8], axis=0, keepdims=True)

    sum_copies = []
    for side in range(2):
        for step in (8, 9, 7, 10, 6, 11, 5, 12, 4, 13, 3, 14, 2, 15, 1, 0):
            if side == 0 and step == 0:
                continue
            copy = pltpu.make_async_remote_copy(
                src_ref=sum_in.at[me],
                dst_ref=sum_in.at[me],
                send_sem=sum_send.at[N * side + step],
                recv_sem=sum_recv.at[N * side + (N - step) % N],
                device_id=plane(side, step),
                device_id_type=MESH,
            )
            copy.start()
            sum_copies.append(copy)
    moved_copy.wait_recv()
    for part, rows in ((half, moved.at[half]), (1 - half, moved_in)):
        for c in range(3):
            for b in range(2):
                for blk in range(4):
                    at = pl.ds(pl.multiple_of(GHOST * part + 128 * blk, 128), 128)
                    row = 8 * c + 4 * b + blk
                    new_pos[c, b : b + 1, at] = rows[row : row + 1, :]
    store(new_pos, pos_hbm_out)
    dense_rows(0, 2)
    for copy in sum_copies:
        copy.wait_recv()
    total = sum_in[0]
    for r in range(1, 2 * N):
        total = total + sum_in[r]
    all_in[0] = total
    all_copies = []
    for step in (4, 3, 5, 2, 6, 1, 7):
        copy = pltpu.make_async_remote_copy(
            src_ref=all_in.at[0],
            dst_ref=all_in.at[RING - step],
            send_sem=all_send.at[step],
            recv_sem=all_recv.at[RING - step],
            device_id={"bead": 2 * lax.rem(ring + step, RING) + half},
            device_id_type=MESH,
        )
        copy.start()
        all_copies.append(copy)
    dense_rows(2, 4)
    for copy in all_copies:
        copy.wait_recv()
    every = jnp.concatenate([all_in[r] for r in range(RING)], axis=0)
    for b in range(2):
        own = jnp.where(half == 0, every[b : b + 1], every[2 + b : 3 + b])
        prod = every * (own * (1.0 / (APD * N)))
        prod = prod + pltpu.roll(prod, 64, 1)
        low = prod if b == 0 else jnp.concatenate([prod[b:], prod[0:b]], axis=0)
        high = jnp.concatenate([prod[b + 2 :], prod[0 : b + 2]], axis=0)
        corr[b] = jnp.where(half == 0, low, high)[:, 0:64]

    store(corr, corr_hbm_out)
    for copy in small + ghosts + pos_copies + force_copies + [moved_copy] + sum_copies + all_copies:
        copy.wait_send()
    for copy in stores:
        copy.wait()


def write_out(feats_in, pos_in, corr_in, feats_out, pos_out, corr_out, sems):
    copies = []
    for source, target in ((feats_in, feats_out), (pos_in, pos_out), (corr_in, corr_out)):
        copy = pltpu.make_async_copy(source, target, sems.at[len(copies)])
        copy.start()
        copies.append(copy)
    for copy in copies:
        copy.wait()


def on_device(
    features, positions, send_rows, neighbours, nbr_mask, w_pair, w_in, w_out, omega, q_index
):
    hbm = pl.BlockSpec(memory_space=pltpu.HBM)
    dma = pltpu.SemaphoreType.DMA
    shapes = (
        jax.ShapeDtypeStruct((2, APD, W), BF16),
        jax.ShapeDtypeStruct((3, 2, APD), F32),
        jax.ShapeDtypeStruct((2, 32, 64), F32),
    )
    results = pl.pallas_call(
        kernel,
        out_shape=shapes,
        in_specs=[hbm] * 10,
        out_specs=(hbm, hbm, hbm),
        scratch_shapes=[
            pltpu.VMEM((2, APD, W), BF16),
            pltpu.VMEM((3, 2, APD), F32),
            pltpu.VMEM((1, 2, GHOST), jnp.int32),
            pltpu.VMEM((SLOTS, APD), jnp.int32),
            pltpu.VMEM((SLOTS, APD), jnp.int32),
            pltpu.VMEM((1, W), BF16),
            pltpu.VMEM((2 * W, 512), BF16),
            pltpu.VMEM((512, W), BF16),
            pltpu.SMEM((2,), F32),
            pltpu.VMEM((3, 64), jnp.int32),
            dma((10,)),
            pltpu.VMEM((2, APD, W), BF16),
            pltpu.VMEM((3, 2, APD), F32),
            pltpu.VMEM((2, 32, 64), F32),
            dma((8,)),
            pltpu.VMEM((8, EXT), F32),
            pltpu.VMEM((2, 8, GHOST), F32),
            pltpu.VMEM((2, 2 * W, GHOST), BF16),
            pltpu.VMEM((2 * W, EXT), BF16),
            pltpu.VMEM((8, SLOTS, APD), F32),
            pltpu.VMEM((3, SLOTS, APD), F32),
            pltpu.VMEM((2, W, APD), F32),
            pltpu.VMEM((2, APD, TILE), BF16),
            pltpu.VMEM((2, 32, 128), F32),
            pltpu.VMEM((N, 32, 128), F32),
            pltpu.VMEM((2, 24, 128), F32),
            pltpu.VMEM((N, 24, 128), F32),
            pltpu.VMEM((2, 32, 128), F32),
            pltpu.VMEM((128, 1024), F32),
            pltpu.VMEM((2, 24, 128), F32),
            pltpu.VMEM((24, 128), F32),
            pltpu.VMEM((2 * N, 4, 128), F32),
            pltpu.VMEM((RING, 4, 128), F32),
            dma((2,)),
            dma((2,)),
            dma((2,)),
            dma((2,)),
            dma((N,)),
            dma((N,)),
            dma((N,)),
            dma((N,)),
            dma((2,)),
            dma((2 * N,)),
            dma((2 * N,)),
            dma((RING,)),
            dma((RING,)),
        ],
        compiler_params=pltpu.CompilerParams(
            collective_id=0, has_side_effects=True, vmem_limit_bytes=64 * 2**20 - 2**17
        ),
    )(
        features,
        jnp.transpose(positions, (1, 0, 2)),
        send_rows,
        neighbours,
        nbr_mask,
        w_pair.reshape(1, W),
        w_in,
        w_out,
        omega,
        q_index,
    )
    new_features, new_positions, correlation = pl.pallas_call(
        write_out,
        out_shape=shapes,
        in_specs=[pl.BlockSpec(memory_space=pltpu.VMEM)] * 3,
        out_specs=(hbm, hbm, hbm),
        scratch_shapes=[dma((3,))],
    )(*results)
    return (new_features, jnp.transpose(new_positions, (1, 0, 2)), correlation)


def solution(mesh):
    in_specs = (
        P("bead", "space", None),
        P("bead", None, "space"),
        P("space", None, None),
        P(None, "space"),
        P(None, "space"),
        P(),
        P(),
        P(),
        P("bead"),
        P(),
    )
    out_specs = (P("bead", "space", None), P("bead", None, "space"), P("bead", None, None))
    return jax.shard_map(
        on_device, mesh=mesh, in_specs=in_specs, out_specs=out_specs, check_vma=False
    )
```

```python
import functools
import math

import jax
import jax.numpy as jnp
from jax import lax
from jax.experimental import pallas as pl
from jax.experimental.pallas import tpu as pltpu
from jax.sharding import PartitionSpec as P

MESH = pl.DeviceIdType.MESH
F32 = jnp.float32
BF16 = jnp.bfloat16
HIGHEST = lax.Precision.HIGHEST
N = 16
RING = 8
APD = 1024
GHOST = 512
EXT = 2048
W = 128
SLOTS = 8
TILE = 256
BOX = 32.0


def other(axis, offset):
    return {axis: lax.rem(lax.axis_index(axis) + offset, N)}


def lane_gather(row, index):
    return jnp.take_along_axis(row, index, axis=1, mode="promise_in_bounds")


def cos_turns(t):
    t = t - jnp.round(t)
    u = (t * t) * (math.pi * math.pi / 4.0)
    m = u * (-0.5 + u * (1.0 / 24 + u * (-1.0 / 720 + u * (1.0 / 40320 - u / 3628800))))
    m = 2.0 * m * (m + 2.0)
    m = 2.0 * m * (m + 2.0)
    return 1.0 + m


def dct_entry(k, bead):
    turns = lax.bitwise_and(k * (2 * bead + 1), 127).astype(F32) * (1.0 / 128.0)
    return jnp.where(k == 0, math.sqrt(1.0 / 32), math.sqrt(2.0 / 32)) * cos_turns(turns)


def kernel(
    feats_hbm,
    pos_hbm,
    send_hbm,
    nbr_hbm,
    mask_hbm,
    w_pair_hbm,
    w_in_hbm,
    w_out_hbm,
    omega_hbm,
    q_hbm,
    feats_hbm_out,
    pos_hbm_out,
    corr_hbm_out,
    feats,
    pos,
    send,
    nbr,
    mask,
    w_pair,
    w_in,
    w_out,
    omega,
    q_index,
    load_sem,
    new_feats,
    new_pos,
    corr,
    store_sem,
    table,
    small_out,
    ghost_out,
    wide_feats,
    picks,
    terms,
    agg_own,
    dense,
    pos_out,
    pos_in,
    force_out,
    force_in,
    waves,
    coeff,
    moved,
    moved_in,
    sum_in,
    all_in,
    small_send,
    small_recv,
    ghost_send,
    ghost_recv,
    pos_send,
    pos_recv,
    force_send,
    force_recv,
    moved_sem,
    sum_send,
    sum_recv,
    all_send,
    all_recv,
):
    bead = lax.axis_index("bead")
    space = lax.axis_index("space")
    ring = lax.div(bead, 2)
    half = lax.rem(bead, 2)
    barrier = pltpu.get_barrier_semaphore()

    def plane(side, step):
        return {
            "bead": 2 * ring + lax.rem(half + side, 2),
            "space": lax.rem(space + step, N),
        }

    loads = []
    for source, target in (
        (w_pair_hbm, w_pair),
        (feats_hbm, feats),
        (pos_hbm, pos),
        (send_hbm, send),
        (nbr_hbm, nbr),
        (mask_hbm, mask),
        (omega_hbm, omega),
        (w_in_hbm, w_in),
        (w_out_hbm, w_out),
        (q_hbm, q_index),
    ):
        copy = pltpu.make_async_copy(source, target, load_sem.at[len(loads)])
        copy.start()
        loads.append(copy)

    for step in (1, N - 1) + tuple(range(2, N - 1)):
        pl.semaphore_signal(barrier, inc=1, device_id=plane(0, step), device_id_type=MESH)
    for step in range(N):
        pl.semaphore_signal(barrier, inc=1, device_id=plane(1, step), device_id_type=MESH)
    for step in range(1, RING):
        for side in range(2):
            to = 2 * lax.rem(ring + step, RING) + side
            pl.semaphore_signal(barrier, inc=1, device_id={"bead": to}, device_id_type=MESH)
    partners = (N - 1) + N + 2 * (RING - 1)

    for i in range(4):
        loads[i].wait()
    pair_rows = jnp.broadcast_to(w_pair[...], (16, W))
    for b in range(2):
        strength = lax.dot_general(
            pair_rows, feats[b], (((1,), (1,)), ((), ())), preferred_element_type=F32
        )
        for c in range(3):
            table[4 * b + c : 4 * b + c + 1, 0:APD] = pos[c, b : b + 1]
        table[4 * b + 3 : 4 * b + 4, 0:APD] = strength[0:1]

    for side in range(2):
        for blk in range(4):
            idx = jnp.broadcast_to(send[0, side : side + 1, 128 * blk : 128 * blk + 128], (8, 128))
            hi = lax.shift_right_logical(idx, 7)
            lo = lax.bitwise_and(idx, 127)
            acc = jnp.zeros((8, 128), F32)
            for h in range(8):
                got = lane_gather(table[:, 128 * h : 128 * h + 128], lo)
                acc = jnp.where(hi == h, got, acc)
            small_out[side, :, 128 * blk : 128 * blk + 128] = acc

    for i in range(4, 7):
        loads[i].wait()
    for part in range(2):
        for c in range(3):
            for b in range(2):
                for blk in range(4):
                    at = GHOST * part + 128 * blk
                    row = 8 * c + 4 * b + blk
                    pos_out[part, row : row + 1] = pos[c, b : b + 1, at : at + 128]
    angle = jnp.concatenate([jnp.full((1, 128), omega[b], F32) for b in range(2)], axis=0)
    wave_rows = jnp.concatenate([jnp.cos(angle), jnp.sin(angle), jnp.zeros((4, 128), F32)], axis=0)
    for part in range(2):
        pos_out[part, 24:32] = wave_rows

    pl.semaphore_wait(barrier, partners)

    def to_neighbour(source, target, send_sem, recv_sem, side):
        copy = pltpu.make_async_remote_copy(
            src_ref=source,
            dst_ref=target,
            send_sem=send_sem.at[side],
            recv_sem=recv_sem.at[side],
            device_id=other("space", N - 1 if side == 0 else 1),
            device_id_type=MESH,
        )
        copy.start()
        return copy

    small = []
    for side in range(2):
        start = APD + GHOST if side == 0 else APD
        small.append(
            to_neighbour(
                small_out.at[side], table.at[:, pl.ds(start, GHOST)], small_send, small_recv, side
            )
        )

    def to_beads(source, target, send_sem, recv_sem, offsets):
        copies = []
        for o in offsets:
            to = lax.rem(bead + o, N)
            copy = pltpu.make_async_remote_copy(
                src_ref=source.at[lax.rem(to, 2)],
                dst_ref=target.at[bead],
                send_sem=send_sem.at[o],
                recv_sem=recv_sem.at[N - o],
                device_id={"bead": to},
                device_id_type=MESH,
            )
            copy.start()
            copies.append(copy)
        return copies

    crossing = (7, 9, 5, 11, 3, 13, 1, 15)
    straight = (8, 6, 10, 4, 12, 2, 14)
    pos_copies = to_beads(pos_out, pos_in, pos_send, pos_recv, crossing + straight)
    pos_in[bead] = pos_out[half]

    for b in range(2):
        for blk in range(APD // 128):
            at = slice(128 * blk, 128 * blk + 128)
            wide_feats[W * b : W * b + W, at] = jnp.transpose(feats[b, at, :])
    tall = lax.broadcasted_iota(jnp.int32, (APD, GHOST), 0)
    for side in range(2):
        hot = (tall == send[0, side : side + 1, :]).astype(F32).astype(BF16)
        ghost_out[side] = jnp.dot(
            wide_feats[:, 0:APD], hot, preferred_element_type=F32
        ).astype(BF16)

    def pick(at, picked, first, last):
        idx = nbr[:, at]
        hi = lax.shift_right_logical(idx, 7)
        lo = lax.bitwise_and(idx, 127)
        for h in range(first, last):
            hit = hi == h
            for q in range(8):
                row = jnp.broadcast_to(table[q : q + 1, 128 * h : 128 * h + 128], (8, 128))
                picked[q] = jnp.where(hit, lane_gather(row, lo), picked[q])
        return picked

    def own_block(blk, _):
        at = pl.ds(pl.multiple_of(128 * blk, 128), 128)
        got = pick(at, [jnp.zeros((8, 128), F32) for _ in range(8)], 0, APD // 128)
        for q in range(8):
            picks[q, :, at] = got[q]
        return 0

    lax.fori_loop(0, APD // 128, own_block, 0)

    for copy in small:
        copy.wait_recv()

    def block(part, blk):
        at = pl.ds(pl.multiple_of(GHOST * part + 128 * blk, 128), 128)
        picked = pick(at, [picks[q, :, at] for q in range(8)], APD // 128, EXT // 128)
        idx = nbr[:, at]
        live = mask[:, at].astype(F32)
        hi = lax.shift_right_logical(idx, 7)
        lo = lax.bitwise_and(idx, 127)
        code = (128 + lo).astype(F32) * lax.shift_left(jnp.ones_like(hi), hi).astype(F32)
        cs = []
        for b in range(2):
            d = []
            for c in range(3):
                d.append(table[4 * b + c : 4 * b + c + 1, at] - picked[4 * b + c])
            first = d[0]
            d[0] = jnp.where(
                first > BOX / 2,
                first - BOX,
                jnp.where(first < -BOX / 2, first + BOX, first),
            )
            dist = d[0] * d[0] + d[1] * d[1] + d[2] * d[2]
            weight = live / (1.0 + dist / 4.0)
            pair = weight * (table[4 * b + 3 : 4 * b + 4, at] + picked[4 * b + 3])
            for c in range(3):
                row = pl.ds(8 * c + 4 * b + blk, 1)
                force_out[part, row, :] = jnp.sum(pair * d[c], axis=0, keepdims=True)
            cs.append(weight)
        total = list(cs)
        for r in range(1, SLOTS):
            same = pltpu.roll(idx, r, 0) == idx
            for b in range(2):
                total[b] = total[b] + jnp.where(same, pltpu.roll(cs[b], r, 0), 0.0)
        terms[0, :, at] = code
        terms[1, :, at] = total[0]
        terms[2, :, at] = total[1]

    def blocks(part):
        def step(blk, _):
            block(part, blk)
            return 0

        lax.fori_loop(0, 4, step, 0)

    blocks(1 - half)
    force_copies = to_beads(force_out, force_in, force_send, force_recv, crossing)
    blocks(half)
    force_copies += to_beads(force_out, force_in, force_send, force_recv, straight)
    force_in[bead] = force_out[half]
    ghosts = []
    for side in range(2):
        start = APD + GHOST if side == 0 else APD
        ghosts.append(
            to_neighbour(
                ghost_out.at[side],
                wide_feats.at[:, pl.ds(start, GHOST)],
                ghost_send,
                ghost_recv,
                side,
            )
        )

    sub_code = (128 + lax.broadcasted_iota(jnp.int32, (32, 128), 0)).astype(F32)

    def dense_half(t, first):
        for blk in range(TILE // 128):
            lanes = slice(128 * blk, 128 * blk + 128)
            at = pl.ds(pl.multiple_of(t * TILE + 128 * blk, 128), 128)

            def spread_row(kind, k):
                return jnp.broadcast_to(terms[kind, k : k + 1, at], (32, 128)).astype(BF16)

            codes, c0, c1 = [[spread_row(kind, k) for k in range(SLOTS)] for kind in range(3)]

            def strip(s, _):
                base = sub_code + (32 * s).astype(F32)
                for h in range(8):
                    here = (base * float(2 ** (first // 128 + h))).astype(BF16)
                    a0 = jnp.zeros((32, 128), BF16)
                    a1 = jnp.zeros((32, 128), BF16)
                    for k in range(SLOTS):
                        hit = codes[k] == here
                        a0 = jnp.where(hit, c0[k], a0)
                        a1 = jnp.where(hit, c1[k], a1)
                    row = pl.ds(pl.multiple_of(128 * h + 32 * s, 32), 32)
                    dense[0, row, lanes] = a0
                    dense[1, row, lanes] = a1
                return 0

            lax.fori_loop(0, 4, strip, 0)
        return [
            jnp.dot(
                wide_feats[W * b : W * b + W, first : first + APD],
                dense[b],
                preferred_element_type=F32,
            )
            for b in range(2)
        ]

    def own_tile(t, _):
        at = pl.ds(pl.multiple_of(t * TILE, TILE), TILE)
        agg_own[0, :, at], agg_own[1, :, at] = dense_half(t, 0)
        return 0

    def dense_tile(t):
        at = pl.ds(pl.multiple_of(t * TILE, TILE), TILE)
        ghost_part = dense_half(t, APD)
        for b in range(2):
            agg = jnp.transpose(agg_own[b, :, at] + ghost_part[b])
            mine = feats[b, at, :]
            joined = jnp.concatenate([mine, agg.astype(BF16)], axis=1)
            x = jnp.dot(joined, w_in[...], preferred_element_type=F32)
            hidden = (x * (0.5 * (1.0 + jnp.tanh(0.5 * x)))).astype(BF16)
            out = mine.astype(F32) + jnp.dot(hidden, w_out[...], preferred_element_type=F32)
            new_feats[b, at, :] = out.astype(BF16)

    def dense_tiles(first, last):
        def step(t, _):
            dense_tile(t)
            return 0

        lax.fori_loop(first, last, step, 0)

    stores = []

    def store(source, target):
        copy = pltpu.make_async_copy(source, target, store_sem.at[len(stores)])
        copy.start()
        stores.append(copy)

    def dense_rows(first, last):
        dense_tiles(first, last)
        for b in range(2):
            rows = pl.ds(first * TILE, (last - first) * TILE)
            store(new_feats.at[b, rows], feats_hbm_out.at[b, rows])

    lax.fori_loop(0, APD // TILE, own_tile, 0)

    for copy in pos_copies:
        copy.wait_recv()
    for source in range(N):
        waves[0, 2 * source : 2 * source + 2] = pos_in[source, 24:26]
        waves[1, 2 * source : 2 * source + 2] = pos_in[source, 26:28]
    k_rows = lax.broadcasted_iota(jnp.int32, (32, 128), 0)
    by_mode = []
    for e in range(4):
        entry = dct_entry(k_rows, 4 * ring + e)
        by_mode += [entry * waves[0], entry * waves[1]]
    rows = lax.broadcasted_iota(jnp.int32, (128, 32), 0)
    source_bead = 2 * lax.shift_right_logical(rows, 3) + lax.bitwise_and(
        lax.shift_right_logical(rows, 2), 1
    )
    spread = dct_entry(lax.broadcasted_iota(jnp.int32, (128, 32), 1), source_bead)
    coeff[...] = jnp.dot(
        spread,
        jnp.concatenate(by_mode, axis=1),
        precision=HIGHEST,
        preferred_element_type=F32,
    )

    def mix(kind, data, acc):
        for source in range(N):
            for c in range(3):
                value = data[source, 8 * c : 8 * c + 8]
                for e in range(4):
                    lanes = slice(128 * (2 * e + kind), 128 * (2 * e + kind) + 128)
                    acc[3 * e + c] = acc[3 * e + c] + coeff[8 * source : 8 * source + 8, lanes] * value
        return acc

    acc = mix(0, pos_in, [jnp.zeros((8, 128), F32) for _ in range(12)])

    for i in range(7, 10):
        loads[i].wait()

    q0 = q_index[0:1, :]
    pick = 4 * (q_index[1:2, :] - 1) + (q_index[2:3, :] - 1)
    pick = jnp.concatenate([pick, pick + 16], axis=1)
    q0 = jnp.concatenate([q0, q0], axis=1)
    row128 = lax.broadcasted_iota(jnp.int32, (128, 128), 0)
    choose = (lax.bitwise_and(row128, 31) == pick).astype(F32)
    row32 = lax.broadcasted_iota(jnp.int32, (32, 128), 0)
    lane32 = lax.broadcasted_iota(jnp.int32, (32, 128), 1)
    row8 = lax.bitwise_and(row32, 7)
    direct = (row8 == q0 - 1).astype(F32)
    crossed = jnp.where(row8 == q0 + 3, jnp.where(lane32 < 64, -1.0, 1.0), 0.0)
    same_bead = lax.shift_right_logical(row32, 3) == lax.shift_right_logical(lane32, 5)
    r8 = lax.broadcasted_iota(jnp.int32, (8, 128), 0)
    u_q = (lax.bitwise_and(r8, 3) + 1).astype(F32) * (1.0 / BOX)
    u_off = jnp.where(r8 >= 4, 0.25, 0.0)
    v_q1 = (lax.bitwise_and(lax.shift_right_logical(row32, 2), 3) + 1).astype(F32) * 0.25
    v_q2 = (lax.bitwise_and(row32, 3) + 1).astype(F32) * 0.25
    v_off = jnp.where(row32 >= 16, 0.25, 0.0)

    for copy in force_copies:
        copy.wait_recv()
    acc = mix(1, force_in, acc)
    for e in range(4):
        for c in range(3):
            row = 8 * c + 4 * (e % 2)
            value = acc[3 * e + c]
            moved[e // 2, row : row + 4] = (value + pltpu.roll(value, 4, 0))[0:4]
    moved_copy = pltpu.make_async_remote_copy(
        src_ref=moved.at[1 - half],
        dst_ref=moved_in,
        send_sem=moved_sem.at[0],
        recv_sem=moved_sem.at[1],
        device_id={"bead": 2 * ring + (1 - half)},
        device_id_type=MESH,
    )
    moved_copy.start()

    us, vs = [], []
    for e in range(4):
        u, v = [], []
        for blk in range(4):
            row = 4 * (e % 2) + blk
            x = moved[e // 2, row : row + 1]
            y = moved[e // 2, 8 + row : 9 + row]
            z = moved[e // 2, 16 + row : 17 + row]
            u.append(cos_turns(u_q * x - u_off))
            v.append(cos_turns(v_q1 * y + v_q2 * z - v_off))
        us.append(jnp.concatenate(u, axis=1))
        vs.append(jnp.concatenate(v, axis=1))
    raw = lax.dot_general(
        jnp.concatenate(us, axis=0),
        jnp.concatenate(vs, axis=0),
        (((1,), (1,)), ((), ())),
        precision=HIGHEST,
        preferred_element_type=F32,
    )
    raw = jnp.where(same_bead, raw, 0.0)
    by_q = jnp.dot(raw, choose, precision=HIGHEST, preferred_element_type=F32)
    parts = direct * by_q + crossed * pltpu.roll(by_q, 64, 1)
    me = N * half + space
    for e in range(4):
        sum_in[me, e : e + 1] = jnp.sum(parts[8 * e : 8 * e + 8], axis=0, keepdims=True)

    sum_copies = []
    for side in (1, 0):
        for step in (8, 9, 7, 10, 6, 11, 5, 12, 4, 13, 3, 14, 2, 15, 1, 0):
            if side == 0 and step == 0:
                continue
            copy = pltpu.make_async_remote_copy(
                src_ref=sum_in.at[me],
                dst_ref=sum_in.at[me],
                send_sem=sum_send.at[N * side + step],
                recv_sem=sum_recv.at[N * side + (N - step) % N],
                device_id=plane(side, step),
                device_id_type=MESH,
            )
            copy.start()
            sum_copies.append(copy)
    moved_copy.wait_recv()
    for part, rows in ((half, moved.at[half]), (1 - half, moved_in)):
        for c in range(3):
            for b in range(2):
                for blk in range(4):
                    at = pl.ds(pl.multiple_of(GHOST * part + 128 * blk, 128), 128)
                    row = 8 * c + 4 * b + blk
                    new_pos[c, b : b + 1, at] = rows[row : row + 1, :]
    store(new_pos, pos_hbm_out)
    for copy in ghosts:
        copy.wait_recv()
    dense_rows(0, 2)
    for copy in sum_copies:
        copy.wait_recv()
    total = sum_in[0]
    for r in range(1, 2 * N):
        total = total + sum_in[r]
    all_in[0] = total
    all_copies = []
    for step in (4, 3, 5, 2, 6, 1, 7):
        copy = pltpu.make_async_remote_copy(
            src_ref=all_in.at[0],
            dst_ref=all_in.at[RING - step],
            send_sem=all_send.at[step],
            recv_sem=all_recv.at[RING - step],
            device_id={"bead": 2 * lax.rem(ring + step, RING) + half},
            device_id_type=MESH,
        )
        copy.start()
        all_copies.append(copy)
    dense_rows(2, 4)
    for copy in all_copies:
        copy.wait_recv()
    every = jnp.concatenate([all_in[r] for r in range(RING)], axis=0)
    for b in range(2):
        own = jnp.where(half == 0, every[b : b + 1], every[2 + b : 3 + b])
        prod = every * (own * (1.0 / (APD * N)))
        prod = prod + pltpu.roll(prod, 64, 1)
        low = prod if b == 0 else jnp.concatenate([prod[b:], prod[0:b]], axis=0)
        high = jnp.concatenate([prod[b + 2 :], prod[0 : b + 2]], axis=0)
        corr[b] = jnp.where(half == 0, low, high)[:, 0:64]

    store(corr, corr_hbm_out)
    for copy in small + ghosts + pos_copies + force_copies + [moved_copy] + sum_copies + all_copies:
        copy.wait_send()
    for copy in stores:
        copy.wait()


def write_out(feats_in, pos_in, corr_in, feats_out, pos_out, corr_out, sems):
    copies = []
    for source, target in ((feats_in, feats_out), (pos_in, pos_out), (corr_in, corr_out)):
        copy = pltpu.make_async_copy(source, target, sems.at[len(copies)])
        copy.start()
        copies.append(copy)
    for copy in copies:
        copy.wait()


def on_device(
    features, positions, send_rows, neighbours, nbr_mask, w_pair, w_in, w_out, omega, q_index
):
    hbm = pl.BlockSpec(memory_space=pltpu.HBM)
    dma = pltpu.SemaphoreType.DMA
    shapes = (
        jax.ShapeDtypeStruct((2, APD, W), BF16),
        jax.ShapeDtypeStruct((3, 2, APD), F32),
        jax.ShapeDtypeStruct((2, 32, 64), F32),
    )
    results = pl.pallas_call(
        kernel,
        out_shape=shapes,
        in_specs=[hbm] * 10,
        out_specs=(hbm, hbm, hbm),
        scratch_shapes=[
            pltpu.VMEM((2, APD, W), BF16),
            pltpu.VMEM((3, 2, APD), F32),
            pltpu.VMEM((1, 2, GHOST), jnp.int32),
            pltpu.VMEM((SLOTS, APD), jnp.int32),
            pltpu.VMEM((SLOTS, APD), jnp.int32),
            pltpu.VMEM((1, W), BF16),
            pltpu.VMEM((2 * W, 512), BF16),
            pltpu.VMEM((512, W), BF16),
            pltpu.SMEM((2,), F32),
            pltpu.VMEM((3, 64), jnp.int32),
            dma((10,)),
            pltpu.VMEM((2, APD, W), BF16),
            pltpu.VMEM((3, 2, APD), F32),
            pltpu.VMEM((2, 32, 64), F32),
            dma((8,)),
            pltpu.VMEM((8, EXT), F32),
            pltpu.VMEM((2, 8, GHOST), F32),
            pltpu.VMEM((2, 2 * W, GHOST), BF16),
            pltpu.VMEM((2 * W, EXT), BF16),
            pltpu.VMEM((8, SLOTS, APD), F32),
            pltpu.VMEM((3, SLOTS, APD), F32),
            pltpu.VMEM((2, W, APD), F32),
            pltpu.VMEM((2, APD, TILE), BF16),
            pltpu.VMEM((2, 32, 128), F32),
            pltpu.VMEM((N, 32, 128), F32),
            pltpu.VMEM((2, 24, 128), F32),
            pltpu.VMEM((N, 24, 128), F32),
            pltpu.VMEM((2, 32, 128), F32),
            pltpu.VMEM((128, 1024), F32),
            pltpu.VMEM((2, 24, 128), F32),
            pltpu.VMEM((24, 128), F32),
            pltpu.VMEM((2 * N, 4, 128), F32),
            pltpu.VMEM((RING, 4, 128), F32),
            dma((2,)),
            dma((2,)),
            dma((2,)),
            dma((2,)),
            dma((N,)),
            dma((N,)),
            dma((N,)),
            dma((N,)),
            dma((2,)),
            dma((2 * N,)),
            dma((2 * N,)),
            dma((RING,)),
            dma((RING,)),
        ],
        compiler_params=pltpu.CompilerParams(
            collective_id=0, has_side_effects=True, vmem_limit_bytes=64 * 2**20 - 2**17
        ),
    )(
        features,
        jnp.transpose(positions, (1, 0, 2)),
        send_rows,
        neighbours,
        nbr_mask,
        w_pair.reshape(1, W),
        w_in,
        w_out,
        omega,
        q_index,
    )
    new_features, new_positions, correlation = pl.pallas_call(
        write_out,
        out_shape=shapes,
        in_specs=[pl.BlockSpec(memory_space=pltpu.VMEM)] * 3,
        out_specs=(hbm, hbm, hbm),
        scratch_shapes=[dma((3,))],
    )(*results)
    return (new_features, jnp.transpose(new_positions, (1, 0, 2)), correlation)


def solution(mesh):
    in_specs = (
        P("bead", "space", None),
        P("bead", None, "space"),
        P("space", None, None),
        P(None, "space"),
        P(None, "space"),
        P(),
        P(),
        P(),
        P("bead"),
        P(),
    )
    out_specs = (P("bead", "space", None), P("bead", None, "space"), P("bead", None, None))
    return jax.shard_map(
        on_device, mesh=mesh, in_specs=in_specs, out_specs=out_specs, check_vma=False
    )
```

```python
import functools
import math

import jax
import jax.numpy as jnp
from jax import lax
from jax.experimental import pallas as pl
from jax.experimental.pallas import tpu as pltpu
from jax.sharding import PartitionSpec as P

MESH = pl.DeviceIdType.MESH
F32 = jnp.float32
BF16 = jnp.bfloat16
HIGHEST = lax.Precision.HIGHEST
N = 16
RING = 8
APD = 1024
GHOST = 512
EXT = 2048
W = 128
SLOTS = 8
TILE = 256
BOX = 32.0


def other(axis, offset):
    return {axis: lax.rem(lax.axis_index(axis) + offset, N)}


def lane_gather(row, index):
    return jnp.take_along_axis(row, index, axis=1, mode="promise_in_bounds")


def cos_turns(t):
    t = t - jnp.round(t)
    u = (t * t) * (math.pi * math.pi / 4.0)
    m = u * (-0.5 + u * (1.0 / 24 + u * (-1.0 / 720 + u * (1.0 / 40320 - u / 3628800))))
    m = 2.0 * m * (m + 2.0)
    m = 2.0 * m * (m + 2.0)
    return 1.0 + m


def dct_entry(k, bead):
    turns = lax.bitwise_and(k * (2 * bead + 1), 127).astype(F32) * (1.0 / 128.0)
    return jnp.where(k == 0, math.sqrt(1.0 / 32), math.sqrt(2.0 / 32)) * cos_turns(turns)


def kernel(
    feats_hbm,
    pos_hbm,
    send_hbm,
    nbr_hbm,
    mask_hbm,
    w_pair_hbm,
    w_in_hbm,
    w_out_hbm,
    omega_hbm,
    q_hbm,
    feats_hbm_out,
    pos_hbm_out,
    corr_hbm_out,
    feats,
    pos,
    send,
    nbr,
    mask,
    w_pair,
    w_in,
    w_out,
    omega,
    q_index,
    load_sem,
    new_feats,
    new_pos,
    corr,
    store_sem,
    table,
    small_out,
    ghost_out,
    wide_feats,
    picks,
    terms,
    agg_own,
    dense,
    pos_out,
    pos_in,
    force_out,
    force_in,
    waves,
    coeff,
    moved,
    moved_in,
    sum_in,
    all_in,
    small_send,
    small_recv,
    ghost_send,
    ghost_recv,
    pos_send,
    pos_recv,
    force_send,
    force_recv,
    moved_sem,
    sum_send,
    sum_recv,
    all_send,
    all_recv,
):
    bead = lax.axis_index("bead")
    space = lax.axis_index("space")
    ring = lax.div(bead, 2)
    half = lax.rem(bead, 2)
    barrier = pltpu.get_barrier_semaphore()

    def plane(side, step):
        return {
            "bead": 2 * ring + lax.rem(half + side, 2),
            "space": lax.rem(space + step, N),
        }

    loads = []
    for source, target in (
        (w_pair_hbm, w_pair),
        (feats_hbm, feats),
        (pos_hbm, pos),
        (send_hbm, send),
        (nbr_hbm, nbr),
        (mask_hbm, mask),
        (omega_hbm, omega),
        (w_in_hbm, w_in),
        (w_out_hbm, w_out),
        (q_hbm, q_index),
    ):
        copy = pltpu.make_async_copy(source, target, load_sem.at[len(loads)])
        copy.start()
        loads.append(copy)

    for step in (1, N - 1) + tuple(range(2, N - 1)):
        pl.semaphore_signal(barrier, inc=1, device_id=plane(0, step), device_id_type=MESH)
    for step in range(N):
        pl.semaphore_signal(barrier, inc=1, device_id=plane(1, step), device_id_type=MESH)
    for step in range(1, RING):
        for side in range(2):
            to = 2 * lax.rem(ring + step, RING) + side
            pl.semaphore_signal(barrier, inc=1, device_id={"bead": to}, device_id_type=MESH)
    partners = (N - 1) + N + 2 * (RING - 1)

    for i in range(4):
        loads[i].wait()
    pair_rows = jnp.broadcast_to(w_pair[...], (16, W))
    for b in range(2):
        strength = lax.dot_general(
            pair_rows, feats[b], (((1,), (1,)), ((), ())), preferred_element_type=F32
        )
        for c in range(3):
            table[4 * b + c : 4 * b + c + 1, 0:APD] = pos[c, b : b + 1]
        table[4 * b + 3 : 4 * b + 4, 0:APD] = strength[0:1]

    for side in range(2):
        for blk in range(4):
            idx = jnp.broadcast_to(send[0, side : side + 1, 128 * blk : 128 * blk + 128], (8, 128))
            hi = lax.shift_right_logical(idx, 7)
            lo = lax.bitwise_and(idx, 127)
            acc = jnp.zeros((8, 128), F32)
            for h in range(8):
                got = lane_gather(table[:, 128 * h : 128 * h + 128], lo)
                acc = jnp.where(hi == h, got, acc)
            small_out[side, :, 128 * blk : 128 * blk + 128] = acc

    for i in range(4, 7):
        loads[i].wait()
    for part in range(2):
        for c in range(3):
            for b in range(2):
                for blk in range(4):
                    at = GHOST * part + 128 * blk
                    row = 8 * c + 4 * b + blk
                    pos_out[part, row : row + 1] = pos[c, b : b + 1, at : at + 128]
    angle = jnp.concatenate([jnp.full((1, 128), omega[b], F32) for b in range(2)], axis=0)
    wave_rows = jnp.concatenate([jnp.cos(angle), jnp.sin(angle), jnp.zeros((4, 128), F32)], axis=0)
    for part in range(2):
        pos_out[part, 24:32] = wave_rows

    pl.semaphore_wait(barrier, partners)

    def to_neighbour(source, target, send_sem, recv_sem, side):
        copy = pltpu.make_async_remote_copy(
            src_ref=source,
            dst_ref=target,
            send_sem=send_sem.at[side],
            recv_sem=recv_sem.at[side],
            device_id=other("space", N - 1 if side == 0 else 1),
            device_id_type=MESH,
        )
        copy.start()
        return copy

    small = []
    for side in range(2):
        start = APD + GHOST if side == 0 else APD
        small.append(
            to_neighbour(
                small_out.at[side], table.at[:, pl.ds(start, GHOST)], small_send, small_recv, side
            )
        )

    def to_beads(source, target, send_sem, recv_sem, offsets):
        copies = []
        for o in offsets:
            to = lax.rem(bead + o, N)
            copy = pltpu.make_async_remote_copy(
                src_ref=source.at[lax.rem(to, 2)],
                dst_ref=target.at[bead],
                send_sem=send_sem.at[o],
                recv_sem=recv_sem.at[N - o],
                device_id={"bead": to},
                device_id_type=MESH,
            )
            copy.start()
            copies.append(copy)
        return copies

    crossing = (7, 9, 5, 11, 3, 13, 1, 15)
    straight = (8, 6, 10, 4, 12, 2, 14)
    pos_copies = to_beads(pos_out, pos_in, pos_send, pos_recv, crossing + straight)
    pos_in[bead] = pos_out[half]

    for b in range(2):
        for blk in range(APD // 128):
            at = slice(128 * blk, 128 * blk + 128)
            wide_feats[W * b : W * b + W, at] = jnp.transpose(feats[b, at, :])
    tall = lax.broadcasted_iota(jnp.int32, (APD, GHOST), 0)
    for side in range(2):
        hot = (tall == send[0, side : side + 1, :]).astype(F32).astype(BF16)
        ghost_out[side] = jnp.dot(
            wide_feats[:, 0:APD], hot, preferred_element_type=F32
        ).astype(BF16)

    def pick(at, picked, first, last):
        idx = nbr[:, at]
        hi = lax.shift_right_logical(idx, 7)
        lo = lax.bitwise_and(idx, 127)
        for h in range(first, last):
            hit = hi == h
            for q in range(8):
                row = jnp.broadcast_to(table[q : q + 1, 128 * h : 128 * h + 128], (8, 128))
                picked[q] = jnp.where(hit, lane_gather(row, lo), picked[q])
        return picked

    def own_block(blk, _):
        at = pl.ds(pl.multiple_of(128 * blk, 128), 128)
        got = pick(at, [jnp.zeros((8, 128), F32) for _ in range(8)], 0, APD // 128)
        for q in range(8):
            picks[q, :, at] = got[q]
        return 0

    lax.fori_loop(0, APD // 128, own_block, 0)

    for copy in small:
        copy.wait_recv()

    def block(part, blk):
        at = pl.ds(pl.multiple_of(GHOST * part + 128 * blk, 128), 128)
        picked = pick(at, [picks[q, :, at] for q in range(8)], APD // 128, EXT // 128)
        live = mask[:, at].astype(F32)
        cs = []
        for b in range(2):
            d = []
            for c in range(3):
                d.append(table[4 * b + c : 4 * b + c + 1, at] - picked[4 * b + c])
            first = d[0]
            d[0] = jnp.where(
                first > BOX / 2,
                first - BOX,
                jnp.where(first < -BOX / 2, first + BOX, first),
            )
            dist = d[0] * d[0] + d[1] * d[1] + d[2] * d[2]
            weight = live / (1.0 + dist / 4.0)
            pair = weight * (table[4 * b + 3 : 4 * b + 4, at] + picked[4 * b + 3])
            for c in range(3):
                row = pl.ds(8 * c + 4 * b + blk, 1)
                force_out[part, row, :] = jnp.sum(pair * d[c], axis=0, keepdims=True)
            cs.append(weight)
        terms[1, :, at] = cs[0]
        terms[2, :, at] = cs[1]

    def blocks(part):
        def step(blk, _):
            block(part, blk)
            return 0

        lax.fori_loop(0, 4, step, 0)

    blocks(1 - half)
    force_copies = to_beads(force_out, force_in, force_send, force_recv, crossing)
    blocks(half)
    force_copies += to_beads(force_out, force_in, force_send, force_recv, straight)
    force_in[bead] = force_out[half]
    ghosts = []
    for side in range(2):
        start = APD + GHOST if side == 0 else APD
        ghosts.append(
            to_neighbour(
                ghost_out.at[side],
                wide_feats.at[:, pl.ds(start, GHOST)],
                ghost_send,
                ghost_recv,
                side,
            )
        )

    def merge(blk, _):
        at = pl.ds(pl.multiple_of(128 * blk, 128), 128)
        idx = nbr[:, at]
        hi = lax.shift_right_logical(idx, 7)
        lo = lax.bitwise_and(idx, 127)
        terms[0, :, at] = (128 + lo).astype(F32) * lax.shift_left(
            jnp.ones_like(hi), hi
        ).astype(F32)
        single = [terms[1 + b, :, at] for b in range(2)]
        total = list(single)
        for r in range(1, SLOTS):
            same = pltpu.roll(idx, r, 0) == idx
            for b in range(2):
                total[b] = total[b] + jnp.where(same, pltpu.roll(single[b], r, 0), 0.0)
        for b in range(2):
            terms[1 + b, :, at] = total[b]
        return 0

    lax.fori_loop(0, APD // 128, merge, 0)

    sub_code = (128 + lax.broadcasted_iota(jnp.int32, (32, 128), 0)).astype(F32)

    def dense_half(t, first):
        for blk in range(TILE // 128):
            lanes = slice(128 * blk, 128 * blk + 128)
            at = pl.ds(pl.multiple_of(t * TILE + 128 * blk, 128), 128)

            def spread_row(kind, k):
                return jnp.broadcast_to(terms[kind, k : k + 1, at], (32, 128)).astype(BF16)

            codes, c0, c1 = [[spread_row(kind, k) for k in range(SLOTS)] for kind in range(3)]

            def strip(s, _):
                base = sub_code + (32 * s).astype(F32)
                for h in range(8):
                    here = (base * float(2 ** (first // 128 + h))).astype(BF16)
                    a0 = jnp.zeros((32, 128), BF16)
                    a1 = jnp.zeros((32, 128), BF16)
                    for k in range(SLOTS):
                        hit = codes[k] == here
                        a0 = jnp.where(hit, c0[k], a0)
                        a1 = jnp.where(hit, c1[k], a1)
                    row = pl.ds(pl.multiple_of(128 * h + 32 * s, 32), 32)
                    dense[0, row, lanes] = a0
                    dense[1, row, lanes] = a1
                return 0

            lax.fori_loop(0, 4, strip, 0)
        return [
            jnp.dot(
                wide_feats[W * b : W * b + W, first : first + APD],
                dense[b],
                preferred_element_type=F32,
            )
            for b in range(2)
        ]

    def own_tile(t, _):
        at = pl.ds(pl.multiple_of(t * TILE, TILE), TILE)
        agg_own[0, :, at], agg_own[1, :, at] = dense_half(t, 0)
        return 0

    def dense_tile(t):
        at = pl.ds(pl.multiple_of(t * TILE, TILE), TILE)
        ghost_part = dense_half(t, APD)
        for b in range(2):
            agg = jnp.transpose(agg_own[b, :, at] + ghost_part[b])
            mine = feats[b, at, :]
            joined = jnp.concatenate([mine, agg.astype(BF16)], axis=1)
            x = jnp.dot(joined, w_in[...], preferred_element_type=F32)
            hidden = (x * (0.5 * (1.0 + jnp.tanh(0.5 * x)))).astype(BF16)
            out = mine.astype(F32) + jnp.dot(hidden, w_out[...], preferred_element_type=F32)
            new_feats[b, at, :] = out.astype(BF16)

    def dense_tiles(first, last):
        def step(t, _):
            dense_tile(t)
            return 0

        lax.fori_loop(first, last, step, 0)

    stores = []

    def store(source, target):
        copy = pltpu.make_async_copy(source, target, store_sem.at[len(stores)])
        copy.start()
        stores.append(copy)

    def dense_rows(first, last):
        dense_tiles(first, last)
        for b in range(2):
            rows = pl.ds(first * TILE, (last - first) * TILE)
            store(new_feats.at[b, rows], feats_hbm_out.at[b, rows])

    lax.fori_loop(0, APD // TILE, own_tile, 0)

    for copy in pos_copies:
        copy.wait_recv()
    for source in range(N):
        waves[0, 2 * source : 2 * source + 2] = pos_in[source, 24:26]
        waves[1, 2 * source : 2 * source + 2] = pos_in[source, 26:28]
    k_rows = lax.broadcasted_iota(jnp.int32, (32, 128), 0)
    by_mode = []
    for e in range(4):
        entry = dct_entry(k_rows, 4 * ring + e)
        by_mode += [entry * waves[0], entry * waves[1]]
    rows = lax.broadcasted_iota(jnp.int32, (128, 32), 0)
    source_bead = 2 * lax.shift_right_logical(rows, 3) + lax.bitwise_and(
        lax.shift_right_logical(rows, 2), 1
    )
    spread = dct_entry(lax.broadcasted_iota(jnp.int32, (128, 32), 1), source_bead)
    coeff[...] = jnp.dot(
        spread,
        jnp.concatenate(by_mode, axis=1),
        precision=HIGHEST,
        preferred_element_type=F32,
    )

    def mix(kind, data, acc):
        for source in range(N):
            for c in range(3):
                value = data[source, 8 * c : 8 * c + 8]
                for e in range(4):
                    lanes = slice(128 * (2 * e + kind), 128 * (2 * e + kind) + 128)
                    acc[3 * e + c] = acc[3 * e + c] + coeff[8 * source : 8 * source + 8, lanes] * value
        return acc

    acc = mix(0, pos_in, [jnp.zeros((8, 128), F32) for _ in range(12)])

    for i in range(7, 10):
        loads[i].wait()

    q0 = q_index[0:1, :]
    pick = 4 * (q_index[1:2, :] - 1) + (q_index[2:3, :] - 1)
    pick = jnp.concatenate([pick, pick + 16], axis=1)
    q0 = jnp.concatenate([q0, q0], axis=1)
    row128 = lax.broadcasted_iota(jnp.int32, (128, 128), 0)
    choose = (lax.bitwise_and(row128, 31) == pick).astype(F32)
    row32 = lax.broadcasted_iota(jnp.int32, (32, 128), 0)
    lane32 = lax.broadcasted_iota(jnp.int32, (32, 128), 1)
    row8 = lax.bitwise_and(row32, 7)
    direct = (row8 == q0 - 1).astype(F32)
    crossed = jnp.where(row8 == q0 + 3, jnp.where(lane32 < 64, -1.0, 1.0), 0.0)
    same_bead = lax.shift_right_logical(row32, 3) == lax.shift_right_logical(lane32, 5)
    r8 = lax.broadcasted_iota(jnp.int32, (8, 128), 0)
    u_q = (lax.bitwise_and(r8, 3) + 1).astype(F32) * (1.0 / BOX)
    u_off = jnp.where(r8 >= 4, 0.25, 0.0)
    v_q1 = (lax.bitwise_and(lax.shift_right_logical(row32, 2), 3) + 1).astype(F32) * 0.25
    v_q2 = (lax.bitwise_and(row32, 3) + 1).astype(F32) * 0.25
    v_off = jnp.where(row32 >= 16, 0.25, 0.0)

    for copy in force_copies:
        copy.wait_recv()
    acc = mix(1, force_in, acc)
    for e in range(4):
        for c in range(3):
            row = 8 * c + 4 * (e % 2)
            value = acc[3 * e + c]
            moved[e // 2, row : row + 4] = (value + pltpu.roll(value, 4, 0))[0:4]
    moved_copy = pltpu.make_async_remote_copy(
        src_ref=moved.at[1 - half],
        dst_ref=moved_in,
        send_sem=moved_sem.at[0],
        recv_sem=moved_sem.at[1],
        device_id={"bead": 2 * ring + (1 - half)},
        device_id_type=MESH,
    )
    moved_copy.start()

    us, vs = [], []
    for e in range(4):
        u, v = [], []
        for blk in range(4):
            row = 4 * (e % 2) + blk
            x = moved[e // 2, row : row + 1]
            y = moved[e // 2, 8 + row : 9 + row]
            z = moved[e // 2, 16 + row : 17 + row]
            u.append(cos_turns(u_q * x - u_off))
            v.append(cos_turns(v_q1 * y + v_q2 * z - v_off))
        us.append(jnp.concatenate(u, axis=1))
        vs.append(jnp.concatenate(v, axis=1))
    u = jnp.concatenate(us, axis=0)
    v = jnp.concatenate(vs, axis=0)
    u_high, v_high = u.astype(BF16), v.astype(BF16)
    u_low = (u - u_high.astype(F32)).astype(BF16)
    v_low = (v - v_high.astype(F32)).astype(BF16)
    raw = lax.dot_general(
        jnp.concatenate([u_high, u_high, u_low], axis=1),
        jnp.concatenate([v_high, v_low, v_high], axis=1),
        (((1,), (1,)), ((), ())),
        preferred_element_type=F32,
    )
    raw = jnp.where(same_bead, raw, 0.0)
    by_q = jnp.dot(raw, choose, precision=HIGHEST, preferred_element_type=F32)
    parts = direct * by_q + crossed * pltpu.roll(by_q, 64, 1)
    me = N * half + space
    for e in range(4):
        sum_in[me, e : e + 1] = jnp.sum(parts[8 * e : 8 * e + 8], axis=0, keepdims=True)

    sum_copies = []
    for side in (1, 0):
        for step in (8, 9, 7, 10, 6, 11, 5, 12, 4, 13, 3, 14, 2, 15, 1, 0):
            if side == 0 and step == 0:
                continue
            copy = pltpu.make_async_remote_copy(
                src_ref=sum_in.at[me],
                dst_ref=sum_in.at[me],
                send_sem=sum_send.at[N * side + step],
                recv_sem=sum_recv.at[N * side + (N - step) % N],
                device_id=plane(side, step),
                device_id_type=MESH,
            )
            copy.start()
            sum_copies.append(copy)
    moved_copy.wait_recv()
    for part, rows in ((half, moved.at[half]), (1 - half, moved_in)):
        for c in range(3):
            for b in range(2):
                for blk in range(4):
                    at = pl.ds(pl.multiple_of(GHOST * part + 128 * blk, 128), 128)
                    row = 8 * c + 4 * b + blk
                    new_pos[c, b : b + 1, at] = rows[row : row + 1, :]
    store(new_pos, pos_hbm_out)
    for copy in ghosts:
        copy.wait_recv()
    dense_rows(0, 2)
    for copy in sum_copies:
        copy.wait_recv()
    total = sum_in[0]
    for r in range(1, 2 * N):
        total = total + sum_in[r]
    all_in[0] = total
    all_copies = []
    for step in (4, 3, 5, 2, 6, 1, 7):
        copy = pltpu.make_async_remote_copy(
            src_ref=all_in.at[0],
            dst_ref=all_in.at[RING - step],
            send_sem=all_send.at[step],
            recv_sem=all_recv.at[RING - step],
            device_id={"bead": 2 * lax.rem(ring + step, RING) + half},
            device_id_type=MESH,
        )
        copy.start()
        all_copies.append(copy)
    dense_rows(2, 4)
    for copy in all_copies:
        copy.wait_recv()
    every = jnp.concatenate([all_in[r] for r in range(RING)], axis=0)
    for b in range(2):
        own = jnp.where(half == 0, every[b : b + 1], every[2 + b : 3 + b])
        prod = every * (own * (1.0 / (APD * N)))
        prod = prod + pltpu.roll(prod, 64, 1)
        low = prod if b == 0 else jnp.concatenate([prod[b:], prod[0:b]], axis=0)
        high = jnp.concatenate([prod[b + 2 :], prod[0 : b + 2]], axis=0)
        corr[b] = jnp.where(half == 0, low, high)[:, 0:64]

    store(corr, corr_hbm_out)
    for copy in small + ghosts + pos_copies + force_copies + [moved_copy] + sum_copies + all_copies:
        copy.wait_send()
    for copy in stores:
        copy.wait()


def write_out(feats_in, pos_in, corr_in, feats_out, pos_out, corr_out, sems):
    copies = []
    for source, target in ((feats_in, feats_out), (pos_in, pos_out), (corr_in, corr_out)):
        copy = pltpu.make_async_copy(source, target, sems.at[len(copies)])
        copy.start()
        copies.append(copy)
    for copy in copies:
        copy.wait()


def on_device(
    features, positions, send_rows, neighbours, nbr_mask, w_pair, w_in, w_out, omega, q_index
):
    hbm = pl.BlockSpec(memory_space=pltpu.HBM)
    dma = pltpu.SemaphoreType.DMA
    shapes = (
        jax.ShapeDtypeStruct((2, APD, W), BF16),
        jax.ShapeDtypeStruct((3, 2, APD), F32),
        jax.ShapeDtypeStruct((2, 32, 64), F32),
    )
    results = pl.pallas_call(
        kernel,
        out_shape=shapes,
        in_specs=[hbm] * 10,
        out_specs=(hbm, hbm, hbm),
        scratch_shapes=[
            pltpu.VMEM((2, APD, W), BF16),
            pltpu.VMEM((3, 2, APD), F32),
            pltpu.VMEM((1, 2, GHOST), jnp.int32),
            pltpu.VMEM((SLOTS, APD), jnp.int32),
            pltpu.VMEM((SLOTS, APD), jnp.int32),
            pltpu.VMEM((1, W), BF16),
            pltpu.VMEM((2 * W, 512), BF16),
            pltpu.VMEM((512, W), BF16),
            pltpu.SMEM((2,), F32),
            pltpu.VMEM((3, 64), jnp.int32),
            dma((10,)),
            pltpu.VMEM((2, APD, W), BF16),
            pltpu.VMEM((3, 2, APD), F32),
            pltpu.VMEM((2, 32, 64), F32),
            dma((8,)),
            pltpu.VMEM((8, EXT), F32),
            pltpu.VMEM((2, 8, GHOST), F32),
            pltpu.VMEM((2, 2 * W, GHOST), BF16),
            pltpu.VMEM((2 * W, EXT), BF16),
            pltpu.VMEM((8, SLOTS, APD), F32),
            pltpu.VMEM((3, SLOTS, APD), F32),
            pltpu.VMEM((2, W, APD), F32),
            pltpu.VMEM((2, APD, TILE), BF16),
            pltpu.VMEM((2, 32, 128), F32),
            pltpu.VMEM((N, 32, 128), F32),
            pltpu.VMEM((2, 24, 128), F32),
            pltpu.VMEM((N, 24, 128), F32),
            pltpu.VMEM((2, 32, 128), F32),
            pltpu.VMEM((128, 1024), F32),
            pltpu.VMEM((2, 24, 128), F32),
            pltpu.VMEM((24, 128), F32),
            pltpu.VMEM((2 * N, 4, 128), F32),
            pltpu.VMEM((RING, 4, 128), F32),
            dma((2,)),
            dma((2,)),
            dma((2,)),
            dma((2,)),
            dma((N,)),
            dma((N,)),
            dma((N,)),
            dma((N,)),
            dma((2,)),
            dma((2 * N,)),
            dma((2 * N,)),
            dma((RING,)),
            dma((RING,)),
        ],
        compiler_params=pltpu.CompilerParams(
            collective_id=0, has_side_effects=True, vmem_limit_bytes=64 * 2**20 - 2**17
        ),
    )(
        features,
        jnp.transpose(positions, (1, 0, 2)),
        send_rows,
        neighbours,
        nbr_mask,
        w_pair.reshape(1, W),
        w_in,
        w_out,
        omega,
        q_index,
    )
    new_features, new_positions, correlation = pl.pallas_call(
        write_out,
        out_shape=shapes,
        in_specs=[pl.BlockSpec(memory_space=pltpu.VMEM)] * 3,
        out_specs=(hbm, hbm, hbm),
        scratch_shapes=[dma((3,))],
    )(*results)
    return (new_features, jnp.transpose(new_positions, (1, 0, 2)), correlation)


def solution(mesh):
    in_specs = (
        P("bead", "space", None),
        P("bead", None, "space"),
        P("space", None, None),
        P(None, "space"),
        P(None, "space"),
        P(),
        P(),
        P(),
        P("bead"),
        P(),
    )
    out_specs = (P("bead", "space", None), P("bead", None, "space"), P("bead", None, None))
    return jax.shard_map(
        on_device, mesh=mesh, in_specs=in_specs, out_specs=out_specs, check_vma=False
    )
```

```python
import functools
import math

import jax
import jax.numpy as jnp
from jax import lax
from jax.experimental import pallas as pl
from jax.experimental.pallas import tpu as pltpu
from jax.sharding import PartitionSpec as P

MESH = pl.DeviceIdType.MESH
F32 = jnp.float32
BF16 = jnp.bfloat16
HIGHEST = lax.Precision.HIGHEST
N = 16
RING = 8
APD = 1024
GHOST = 512
EXT = 2048
W = 128
SLOTS = 8
TILE = 256
BOX = 32.0


def other(axis, offset):
    return {axis: lax.rem(lax.axis_index(axis) + offset, N)}


def lane_gather(row, index):
    return jnp.take_along_axis(row, index, axis=1, mode="promise_in_bounds")


def cos_turns(t):
    t = t - jnp.round(t)
    u = (t * t) * (math.pi * math.pi / 4.0)
    m = u * (-0.5 + u * (1.0 / 24 + u * (-1.0 / 720 + u * (1.0 / 40320 - u / 3628800))))
    m = 2.0 * m * (m + 2.0)
    m = 2.0 * m * (m + 2.0)
    return 1.0 + m


def dct_entry(k, bead):
    turns = lax.bitwise_and(k * (2 * bead + 1), 127).astype(F32) * (1.0 / 128.0)
    return jnp.where(k == 0, math.sqrt(1.0 / 32), math.sqrt(2.0 / 32)) * cos_turns(turns)


def kernel(
    feats_hbm,
    pos_hbm,
    send_hbm,
    nbr_hbm,
    mask_hbm,
    w_pair_hbm,
    w_in_hbm,
    w_out_hbm,
    omega_hbm,
    q_hbm,
    feats_hbm_out,
    pos_hbm_out,
    corr_hbm_out,
    feats,
    pos,
    send,
    nbr,
    mask,
    w_pair,
    w_in,
    w_out,
    omega,
    q_index,
    load_sem,
    new_feats,
    new_pos,
    corr,
    store_sem,
    table,
    small_out,
    ghost_out,
    wide_feats,
    picks,
    terms,
    agg_own,
    dense,
    pos_out,
    pos_in,
    force_out,
    force_in,
    waves,
    coeff,
    moved,
    moved_in,
    sum_in,
    all_in,
    small_send,
    small_recv,
    ghost_send,
    ghost_recv,
    pos_send,
    pos_recv,
    force_send,
    force_recv,
    moved_sem,
    sum_send,
    sum_recv,
    all_send,
    all_recv,
):
    bead = lax.axis_index("bead")
    space = lax.axis_index("space")
    ring = lax.div(bead, 2)
    half = lax.rem(bead, 2)
    barrier = pltpu.get_barrier_semaphore()

    def plane(side, step):
        return {
            "bead": 2 * ring + lax.rem(half + side, 2),
            "space": lax.rem(space + step, N),
        }

    loads = []
    for source, target in (
        (w_pair_hbm, w_pair),
        (feats_hbm, feats),
        (pos_hbm, pos),
        (send_hbm, send),
        (nbr_hbm, nbr),
        (mask_hbm, mask),
        (omega_hbm, omega),
        (w_in_hbm, w_in),
        (w_out_hbm, w_out),
        (q_hbm, q_index),
    ):
        copy = pltpu.make_async_copy(source, target, load_sem.at[len(loads)])
        copy.start()
        loads.append(copy)

    for step in (1, N - 1) + tuple(range(2, N - 1)):
        pl.semaphore_signal(barrier, inc=1, device_id=plane(0, step), device_id_type=MESH)
    for step in range(N):
        pl.semaphore_signal(barrier, inc=1, device_id=plane(1, step), device_id_type=MESH)
    for step in range(1, RING):
        for side in range(2):
            to = 2 * lax.rem(ring + step, RING) + side
            pl.semaphore_signal(barrier, inc=1, device_id={"bead": to}, device_id_type=MESH)
    partners = (N - 1) + N + 2 * (RING - 1)

    for i in range(4):
        loads[i].wait()
    pair_rows = jnp.broadcast_to(w_pair[...], (16, W))
    for b in range(2):
        strength = lax.dot_general(
            pair_rows, feats[b], (((1,), (1,)), ((), ())), preferred_element_type=F32
        )
        for c in range(3):
            table[4 * b + c : 4 * b + c + 1, 0:APD] = pos[c, b : b + 1]
        table[4 * b + 3 : 4 * b + 4, 0:APD] = strength[0:1]

    for side in range(2):
        for blk in range(4):
            idx = jnp.broadcast_to(send[0, side : side + 1, 128 * blk : 128 * blk + 128], (8, 128))
            hi = lax.shift_right_logical(idx, 7)
            lo = lax.bitwise_and(idx, 127)
            acc = jnp.zeros((8, 128), F32)
            for h in range(8):
                got = lane_gather(table[:, 128 * h : 128 * h + 128], lo)
                acc = jnp.where(hi == h, got, acc)
            small_out[side, :, 128 * blk : 128 * blk + 128] = acc

    for i in range(4, 7):
        loads[i].wait()
    for part in range(2):
        for c in range(3):
            for b in range(2):
                for blk in range(4):
                    at = GHOST * part + 128 * blk
                    row = 8 * c + 4 * b + blk
                    pos_out[part, row : row + 1] = pos[c, b : b + 1, at : at + 128]
    angle = jnp.concatenate([jnp.full((1, 128), omega[b], F32) for b in range(2)], axis=0)
    wave_rows = jnp.concatenate([jnp.cos(angle), jnp.sin(angle), jnp.zeros((4, 128), F32)], axis=0)
    for part in range(2):
        pos_out[part, 24:32] = wave_rows

    pl.semaphore_wait(barrier, partners)

    def to_neighbour(source, target, send_sem, recv_sem, side):
        copy = pltpu.make_async_remote_copy(
            src_ref=source,
            dst_ref=target,
            send_sem=send_sem.at[side],
            recv_sem=recv_sem.at[side],
            device_id=other("space", N - 1 if side == 0 else 1),
            device_id_type=MESH,
        )
        copy.start()
        return copy

    small = []
    for side in range(2):
        start = APD + GHOST if side == 0 else APD
        small.append(
            to_neighbour(
                small_out.at[side], table.at[:, pl.ds(start, GHOST)], small_send, small_recv, side
            )
        )

    def to_beads(source, target, send_sem, recv_sem, offsets):
        copies = []
        for o in offsets:
            to = lax.rem(bead + o, N)
            copy = pltpu.make_async_remote_copy(
                src_ref=source.at[lax.rem(to, 2)],
                dst_ref=target.at[bead],
                send_sem=send_sem.at[o],
                recv_sem=recv_sem.at[N - o],
                device_id={"bead": to},
                device_id_type=MESH,
            )
            copy.start()
            copies.append(copy)
        return copies

    crossing = (7, 9, 5, 11, 3, 13, 1, 15)
    straight = (8, 6, 10, 4, 12, 2, 14)
    pos_copies = to_beads(pos_out, pos_in, pos_send, pos_recv, crossing + straight)
    pos_in[bead] = pos_out[half]

    for b in range(2):
        for blk in range(APD // 128):
            at = slice(128 * blk, 128 * blk + 128)
            wide_feats[W * b : W * b + W, at] = jnp.transpose(feats[b, at, :])
    tall = lax.broadcasted_iota(jnp.int32, (APD, GHOST), 0)
    for side in range(2):
        hot = (tall == send[0, side : side + 1, :]).astype(F32).astype(BF16)
        ghost_out[side] = jnp.dot(
            wide_feats[:, 0:APD], hot, preferred_element_type=F32
        ).astype(BF16)

    def pick(at, picked, first, last):
        idx = nbr[:, at]
        hi = lax.shift_right_logical(idx, 7)
        lo = lax.bitwise_and(idx, 127)
        for h in range(first, last):
            hit = hi == h
            for q in range(8):
                row = jnp.broadcast_to(table[q : q + 1, 128 * h : 128 * h + 128], (8, 128))
                picked[q] = jnp.where(hit, lane_gather(row, lo), picked[q])
        return picked

    def own_block(blk, _):
        at = pl.ds(pl.multiple_of(128 * blk, 128), 128)
        got = pick(at, [jnp.zeros((8, 128), F32) for _ in range(8)], 0, APD // 128)
        for q in range(8):
            picks[q, :, at] = got[q]
        return 0

    lax.fori_loop(0, APD // 128, own_block, 0)

    for copy in small:
        copy.wait_recv()

    def block(part, blk):
        at = pl.ds(pl.multiple_of(GHOST * part + 128 * blk, 128), 128)
        picked = pick(at, [picks[q, :, at] for q in range(8)], APD // 128, EXT // 128)
        live = mask[:, at].astype(F32)
        cs = []
        for b in range(2):
            d = []
            for c in range(3):
                d.append(table[4 * b + c : 4 * b + c + 1, at] - picked[4 * b + c])
            first = d[0]
            d[0] = jnp.where(
                first > BOX / 2,
                first - BOX,
                jnp.where(first < -BOX / 2, first + BOX, first),
            )
            dist = d[0] * d[0] + d[1] * d[1] + d[2] * d[2]
            weight = live / (1.0 + dist / 4.0)
            pair = weight * (table[4 * b + 3 : 4 * b + 4, at] + picked[4 * b + 3])
            for c in range(3):
                row = pl.ds(8 * c + 4 * b + blk, 1)
                force_out[part, row, :] = jnp.sum(pair * d[c], axis=0, keepdims=True)
            cs.append(weight)
        terms[1, :, at] = cs[0]
        terms[2, :, at] = cs[1]

    def blocks(part):
        def step(blk, _):
            block(part, blk)
            return 0

        lax.fori_loop(0, 4, step, 0)

    blocks(1 - half)
    force_copies = to_beads(force_out, force_in, force_send, force_recv, crossing)
    blocks(half)
    force_copies += to_beads(force_out, force_in, force_send, force_recv, straight)
    force_in[bead] = force_out[half]
    ghosts = []
    for side in range(2):
        start = APD + GHOST if side == 0 else APD
        ghosts.append(
            to_neighbour(
                ghost_out.at[side],
                wide_feats.at[:, pl.ds(start, GHOST)],
                ghost_send,
                ghost_recv,
                side,
            )
        )

    def merge(blk, _):
        at = pl.ds(pl.multiple_of(128 * blk, 128), 128)
        idx = nbr[:, at]
        hi = lax.shift_right_logical(idx, 7)
        lo = lax.bitwise_and(idx, 127)
        terms[0, :, at] = (128 + lo).astype(F32) * lax.shift_left(
            jnp.ones_like(hi), hi
        ).astype(F32)
        single = [terms[1 + b, :, at] for b in range(2)]
        total = list(single)
        for r in range(1, SLOTS):
            same = pltpu.roll(idx, r, 0) == idx
            for b in range(2):
                total[b] = total[b] + jnp.where(same, pltpu.roll(single[b], r, 0), 0.0)
        for b in range(2):
            terms[1 + b, :, at] = total[b]
        return 0

    lax.fori_loop(0, APD // 128, merge, 0)

    sub_code = (128 + lax.broadcasted_iota(jnp.int32, (32, 128), 0)).astype(F32)

    def dense_half(t, first):
        for blk in range(TILE // 128):
            lanes = slice(128 * blk, 128 * blk + 128)
            at = pl.ds(pl.multiple_of(t * TILE + 128 * blk, 128), 128)

            def spread_row(kind, k):
                return jnp.broadcast_to(terms[kind, k : k + 1, at], (32, 128)).astype(BF16)

            codes, c0, c1 = [[spread_row(kind, k) for k in range(SLOTS)] for kind in range(3)]

            def strip(s, _):
                base = sub_code + (32 * s).astype(F32)
                for h in range(8):
                    here = (base * float(2 ** (first // 128 + h))).astype(BF16)
                    a0 = jnp.zeros((32, 128), BF16)
                    a1 = jnp.zeros((32, 128), BF16)
                    for k in range(SLOTS):
                        hit = codes[k] == here
                        a0 = jnp.where(hit, c0[k], a0)
                        a1 = jnp.where(hit, c1[k], a1)
                    row = pl.ds(pl.multiple_of(128 * h + 32 * s, 32), 32)
                    dense[0, row, lanes] = a0
                    dense[1, row, lanes] = a1
                return 0

            lax.fori_loop(0, 4, strip, 0)
        return [
            jnp.dot(
                wide_feats[W * b : W * b + W, first : first + APD],
                dense[b],
                preferred_element_type=F32,
            )
            for b in range(2)
        ]

    def own_tile(t, _):
        at = pl.ds(pl.multiple_of(t * TILE, TILE), TILE)
        agg_own[0, :, at], agg_own[1, :, at] = dense_half(t, 0)
        return 0

    def dense_tile(t):
        at = pl.ds(pl.multiple_of(t * TILE, TILE), TILE)
        ghost_part = dense_half(t, APD)
        mine = jnp.concatenate([feats[b, at, :] for b in range(2)], axis=0)
        agg = jnp.concatenate(
            [jnp.transpose(agg_own[b, :, at] + ghost_part[b]).astype(BF16) for b in range(2)],
            axis=0,
        )
        x = jnp.dot(
            jnp.concatenate([mine, agg], axis=1), w_in[...], preferred_element_type=F32
        )
        hidden = (x * (0.5 * (1.0 + jnp.tanh(0.5 * x)))).astype(BF16)
        out = mine.astype(F32) + jnp.dot(hidden, w_out[...], preferred_element_type=F32)
        for b in range(2):
            new_feats[b, at, :] = out[TILE * b : TILE * b + TILE].astype(BF16)

    def dense_tiles(first, last):
        def step(t, _):
            dense_tile(t)
            return 0

        lax.fori_loop(first, last, step, 0)

    stores = []

    def store(source, target):
        copy = pltpu.make_async_copy(source, target, store_sem.at[len(stores)])
        copy.start()
        stores.append(copy)

    def dense_rows(first, last):
        dense_tiles(first, last)
        for b in range(2):
            rows = pl.ds(first * TILE, (last - first) * TILE)
            store(new_feats.at[b, rows], feats_hbm_out.at[b, rows])

    lax.fori_loop(0, APD // TILE, own_tile, 0)

    for copy in pos_copies:
        copy.wait_recv()
    for source in range(N):
        waves[0, 2 * source : 2 * source + 2] = pos_in[source, 24:26]
        waves[1, 2 * source : 2 * source + 2] = pos_in[source, 26:28]
    k_rows = lax.broadcasted_iota(jnp.int32, (32, 128), 0)
    by_mode = []
    for e in range(4):
        entry = dct_entry(k_rows, 4 * ring + e)
        by_mode += [entry * waves[0], entry * waves[1]]
    rows = lax.broadcasted_iota(jnp.int32, (128, 32), 0)
    source_bead = 2 * lax.shift_right_logical(rows, 3) + lax.bitwise_and(
        lax.shift_right_logical(rows, 2), 1
    )
    spread = dct_entry(lax.broadcasted_iota(jnp.int32, (128, 32), 1), source_bead)
    coeff[...] = jnp.dot(
        spread,
        jnp.concatenate(by_mode, axis=1),
        precision=HIGHEST,
        preferred_element_type=F32,
    )

    def mix(kind, data, acc):
        for source in range(N):
            for c in range(3):
                value = data[source, 8 * c : 8 * c + 8]
                for e in range(4):
                    lanes = slice(128 * (2 * e + kind), 128 * (2 * e + kind) + 128)
                    acc[3 * e + c] = acc[3 * e + c] + coeff[8 * source : 8 * source + 8, lanes] * value
        return acc

    acc = mix(0, pos_in, [jnp.zeros((8, 128), F32) for _ in range(12)])

    for i in range(7, 10):
        loads[i].wait()

    q0 = q_index[0:1, :]
    pick = 4 * (q_index[1:2, :] - 1) + (q_index[2:3, :] - 1)
    pick = jnp.concatenate([pick, pick + 16], axis=1)
    q0 = jnp.concatenate([q0, q0], axis=1)
    row128 = lax.broadcasted_iota(jnp.int32, (128, 128), 0)
    choose = (lax.bitwise_and(row128, 31) == pick).astype(F32)
    row32 = lax.broadcasted_iota(jnp.int32, (32, 128), 0)
    lane32 = lax.broadcasted_iota(jnp.int32, (32, 128), 1)
    row8 = lax.bitwise_and(row32, 7)
    direct = (row8 == q0 - 1).astype(F32)
    crossed = jnp.where(row8 == q0 + 3, jnp.where(lane32 < 64, -1.0, 1.0), 0.0)
    same_bead = lax.shift_right_logical(row32, 3) == lax.shift_right_logical(lane32, 5)
    r8 = lax.broadcasted_iota(jnp.int32, (8, 128), 0)
    u_q = (lax.bitwise_and(r8, 3) + 1).astype(F32) * (1.0 / BOX)
    u_off = jnp.where(r8 >= 4, 0.25, 0.0)
    v_q1 = (lax.bitwise_and(lax.shift_right_logical(row32, 2), 3) + 1).astype(F32) * 0.25
    v_q2 = (lax.bitwise_and(row32, 3) + 1).astype(F32) * 0.25
    v_off = jnp.where(row32 >= 16, 0.25, 0.0)

    for copy in force_copies:
        copy.wait_recv()
    acc = mix(1, force_in, acc)
    for e in range(4):
        for c in range(3):
            row = 8 * c + 4 * (e % 2)
            value = acc[3 * e + c]
            moved[e // 2, row : row + 4] = (value + pltpu.roll(value, 4, 0))[0:4]
    moved_copy = pltpu.make_async_remote_copy(
        src_ref=moved.at[1 - half],
        dst_ref=moved_in,
        send_sem=moved_sem.at[0],
        recv_sem=moved_sem.at[1],
        device_id={"bead": 2 * ring + (1 - half)},
        device_id_type=MESH,
    )
    moved_copy.start()

    us, vs = [], []
    for e in range(4):
        u, v = [], []
        for blk in range(4):
            row = 4 * (e % 2) + blk
            x = moved[e // 2, row : row + 1]
            y = moved[e // 2, 8 + row : 9 + row]
            z = moved[e // 2, 16 + row : 17 + row]
            u.append(cos_turns(u_q * x - u_off))
            v.append(cos_turns(v_q1 * y + v_q2 * z - v_off))
        us.append(jnp.concatenate(u, axis=1))
        vs.append(jnp.concatenate(v, axis=1))
    u = jnp.concatenate(us, axis=0)
    v = jnp.concatenate(vs, axis=0)
    u_high, v_high = u.astype(BF16), v.astype(BF16)
    u_low = (u - u_high.astype(F32)).astype(BF16)
    v_low = (v - v_high.astype(F32)).astype(BF16)
    raw = lax.dot_general(
        jnp.concatenate([u_high, u_high, u_low], axis=1),
        jnp.concatenate([v_high, v_low, v_high], axis=1),
        (((1,), (1,)), ((), ())),
        preferred_element_type=F32,
    )
    raw = jnp.where(same_bead, raw, 0.0)
    by_q = jnp.dot(raw, choose, precision=HIGHEST, preferred_element_type=F32)
    parts = direct * by_q + crossed * pltpu.roll(by_q, 64, 1)
    me = N * half + space
    for e in range(4):
        sum_in[me, e : e + 1] = jnp.sum(parts[8 * e : 8 * e + 8], axis=0, keepdims=True)

    sum_copies = []
    for side in (1, 0):
        for step in (8, 9, 7, 10, 6, 11, 5, 12, 4, 13, 3, 14, 2, 15, 1, 0):
            if side == 0 and step == 0:
                continue
            copy = pltpu.make_async_remote_copy(
                src_ref=sum_in.at[me],
                dst_ref=sum_in.at[me],
                send_sem=sum_send.at[N * side + step],
                recv_sem=sum_recv.at[N * side + (N - step) % N],
                device_id=plane(side, step),
                device_id_type=MESH,
            )
            copy.start()
            sum_copies.append(copy)
    moved_copy.wait_recv()
    for part, rows in ((half, moved.at[half]), (1 - half, moved_in)):
        for c in range(3):
            for b in range(2):
                for blk in range(4):
                    at = pl.ds(pl.multiple_of(GHOST * part + 128 * blk, 128), 128)
                    row = 8 * c + 4 * b + blk
                    new_pos[c, b : b + 1, at] = rows[row : row + 1, :]
    store(new_pos, pos_hbm_out)
    for copy in ghosts:
        copy.wait_recv()
    dense_rows(0, 2)
    for copy in sum_copies:
        copy.wait_recv()
    total = sum_in[0]
    for r in range(1, 2 * N):
        total = total + sum_in[r]
    all_in[0] = total
    all_copies = []
    for step in (4, 3, 5, 2, 6, 1, 7):
        copy = pltpu.make_async_remote_copy(
            src_ref=all_in.at[0],
            dst_ref=all_in.at[RING - step],
            send_sem=all_send.at[step],
            recv_sem=all_recv.at[RING - step],
            device_id={"bead": 2 * lax.rem(ring + step, RING) + half},
            device_id_type=MESH,
        )
        copy.start()
        all_copies.append(copy)
    dense_rows(2, 4)
    for copy in all_copies:
        copy.wait_recv()
    every = jnp.concatenate([all_in[r] for r in range(RING)], axis=0)
    for b in range(2):
        own = jnp.where(half == 0, every[b : b + 1], every[2 + b : 3 + b])
        prod = every * (own * (1.0 / (APD * N)))
        prod = prod + pltpu.roll(prod, 64, 1)
        low = prod if b == 0 else jnp.concatenate([prod[b:], prod[0:b]], axis=0)
        high = jnp.concatenate([prod[b + 2 :], prod[0 : b + 2]], axis=0)
        corr[b] = jnp.where(half == 0, low, high)[:, 0:64]

    store(corr, corr_hbm_out)
    for copy in small + ghosts + pos_copies + force_copies + [moved_copy] + sum_copies + all_copies:
        copy.wait_send()
    for copy in stores:
        copy.wait()


def write_out(feats_in, pos_in, corr_in, feats_out, pos_out, corr_out, sems):
    copies = []
    for source, target in ((feats_in, feats_out), (pos_in, pos_out), (corr_in, corr_out)):
        copy = pltpu.make_async_copy(source, target, sems.at[len(copies)])
        copy.start()
        copies.append(copy)
    for copy in copies:
        copy.wait()


def on_device(
    features, positions, send_rows, neighbours, nbr_mask, w_pair, w_in, w_out, omega, q_index
):
    hbm = pl.BlockSpec(memory_space=pltpu.HBM)
    dma = pltpu.SemaphoreType.DMA
    shapes = (
        jax.ShapeDtypeStruct((2, APD, W), BF16),
        jax.ShapeDtypeStruct((3, 2, APD), F32),
        jax.ShapeDtypeStruct((2, 32, 64), F32),
    )
    results = pl.pallas_call(
        kernel,
        out_shape=shapes,
        in_specs=[hbm] * 10,
        out_specs=(hbm, hbm, hbm),
        scratch_shapes=[
            pltpu.VMEM((2, APD, W), BF16),
            pltpu.VMEM((3, 2, APD), F32),
            pltpu.VMEM((1, 2, GHOST), jnp.int32),
            pltpu.VMEM((SLOTS, APD), jnp.int32),
            pltpu.VMEM((SLOTS, APD), jnp.int32),
            pltpu.VMEM((1, W), BF16),
            pltpu.VMEM((2 * W, 512), BF16),
            pltpu.VMEM((512, W), BF16),
            pltpu.SMEM((2,), F32),
            pltpu.VMEM((3, 64), jnp.int32),
            dma((10,)),
            pltpu.VMEM((2, APD, W), BF16),
            pltpu.VMEM((3, 2, APD), F32),
            pltpu.VMEM((2, 32, 64), F32),
            dma((8,)),
            pltpu.VMEM((8, EXT), F32),
            pltpu.VMEM((2, 8, GHOST), F32),
            pltpu.VMEM((2, 2 * W, GHOST), BF16),
            pltpu.VMEM((2 * W, EXT), BF16),
            pltpu.VMEM((8, SLOTS, APD), F32),
            pltpu.VMEM((3, SLOTS, APD), F32),
            pltpu.VMEM((2, W, APD), F32),
            pltpu.VMEM((2, APD, TILE), BF16),
            pltpu.VMEM((2, 32, 128), F32),
            pltpu.VMEM((N, 32, 128), F32),
            pltpu.VMEM((2, 24, 128), F32),
            pltpu.VMEM((N, 24, 128), F32),
            pltpu.VMEM((2, 32, 128), F32),
            pltpu.VMEM((128, 1024), F32),
            pltpu.VMEM((2, 24, 128), F32),
            pltpu.VMEM((24, 128), F32),
            pltpu.VMEM((2 * N, 4, 128), F32),
            pltpu.VMEM((RING, 4, 128), F32),
            dma((2,)),
            dma((2,)),
            dma((2,)),
            dma((2,)),
            dma((N,)),
            dma((N,)),
            dma((N,)),
            dma((N,)),
            dma((2,)),
            dma((2 * N,)),
            dma((2 * N,)),
            dma((RING,)),
            dma((RING,)),
        ],
        compiler_params=pltpu.CompilerParams(
            collective_id=0, has_side_effects=True, vmem_limit_bytes=64 * 2**20 - 2**17
        ),
    )(
        features,
        jnp.transpose(positions, (1, 0, 2)),
        send_rows,
        neighbours,
        nbr_mask,
        w_pair.reshape(1, W),
        w_in,
        w_out,
        omega,
        q_index,
    )
    new_features, new_positions, correlation = pl.pallas_call(
        write_out,
        out_shape=shapes,
        in_specs=[pl.BlockSpec(memory_space=pltpu.VMEM)] * 3,
        out_specs=(hbm, hbm, hbm),
        scratch_shapes=[dma((3,))],
    )(*results)
    return (new_features, jnp.transpose(new_positions, (1, 0, 2)), correlation)


def solution(mesh):
    in_specs = (
        P("bead", "space", None),
        P("bead", None, "space"),
        P("space", None, None),
        P(None, "space"),
        P(None, "space"),
        P(),
        P(),
        P(),
        P("bead"),
        P(),
    )
    out_specs = (P("bead", "space", None), P("bead", None, "space"), P("bead", None, None))
    return jax.shard_map(
        on_device, mesh=mesh, in_specs=in_specs, out_specs=out_specs, check_vma=False
    )
```
